32 devices in a mesh: dp: 4 (over z), expert: 8 (over y, x, core).
Axes of the slice: x: 2, y: 2, z: 4, core: 2. Of those that a mesh axis runs over, the one named last changes fastest.
Arguments:
- hidden_in: bfloat16 [128, 5120], P(('dp', 'expert')), may hold values from -6 to 6
- query: bfloat16 [128, 36864], P(('dp', 'expert')), may hold values from -6 to 24
- prefix_pool: bfloat16 [64, 36864], P('dp'), may hold values from -6 to 6
- suffix_cache: bfloat16 [128, 73728], P(('dp', 'expert')), may hold values from -6 to 6
- block_list: int32 [128, 16], P(('dp', 'expert')), may hold values from 0 to 63, as said below
- prefix_count: int32 [128], P(('dp', 'expert')), may hold values from 1 to 16
- suffix_count: int32 [128], P(('dp', 'expert')), may hold values from 1 to 128
- value_up: bfloat16 [64, 512, 128], P('expert'), may hold values from -0.25 to 0.25
- out_proj: bfloat16 [8192, 5120], P('expert'), may hold values from -0.5 to 0.5
- norm_gain: bfloat16 [5120], replicated, may hold values from 0.5 to 1.5
- expert_ids: int32 [128, 6], P(('dp', 'expert')), may hold values from 0 to 7, all different within a row; in each aligned block of 4 rows (0 to 3, 4 to 7, ...) at most 3 rows name the same one
- gate_weights: bfloat16 [128, 6], P(('dp', 'expert')), may hold values from 0.049804688 to 1
- gate_proj: bfloat16 [8, 5120, 1536], P('expert', None, 'dp'), may hold values from -0.078125 to 0.078125
- up_proj: bfloat16 [8, 5120, 1536], P('expert', None, 'dp'), may hold values from -0.078125 to 0.078125
- down_proj: bfloat16 [8, 1536, 5120], P('expert', 'dp'), may hold values from -0.15625 to 0.15625
Outputs:
- residual_out: float32 [128, 5120], P(('dp', 'expert'))
- moe_out: float32 [128, 5120], P(('dp', 'expert'))
The draws below stay inside these ranges and needn't reach their ends.
Inputs may be any that keep to these rules, and one draw needn't show every extreme that they name: `block_list`: each list names 16 distinct blocks; the lists form a prefix tree: two requests with the same block at a position have the same blocks at all earlier positions. `expert_ids`: each row names 6 different experts; among the rows of one device no expert is named more than 3 times.
All inputs are finite; a program needn't handle non-finite values.
Results may differ from the reference program's by a relative error of at most 0.025.
Values may be sent and summed in bfloat16 or wider, within the bound.
No kernel may reach another device: no remote copies, remote signals or barrier semaphores. Data moves between devices by JAX's collectives and lax.ppermute only.
A program may use at most 128 MiB of HBM per device.

```python
import math
import jax
import jax.numpy as jnp
import numpy as np
from jax import lax

D = 5120
HEADS = 64
LAT = 512
VH = 128
FF = 1536
TOPK = 6
BLOCK = 64
REQ_DEV = 4
SUFFIX = 128
KDIM = 576
TOKENS = 128
NBLK = 64
NB = 16
EXPERTS = 8
CAP = 3
FF_GROUP = 384
N_DP = 4


def draw_query(key, part):
    values = jax.random.normal(key, (TOKENS, HEADS, KDIM), jnp.float32)
    values = jnp.clip(values, -6.0, 24.0)
    return values.reshape(TOKENS, HEADS * KDIM).astype(jnp.bfloat16)


def draw_prefix_pool(key, part):
    values = jax.random.normal(key, (NBLK, BLOCK * KDIM), jnp.float32)
    return jnp.clip(values, -6.0, 6.0).astype(jnp.bfloat16)


def draw_suffix_cache(key, part):
    values = jax.random.normal(key, (TOKENS, SUFFIX * KDIM), jnp.float32)
    return jnp.clip(values, -6.0, 6.0).astype(jnp.bfloat16)


def draw_block_list(key, part):
    ordering = jax.random.permutation(jax.random.fold_in(key, 3), NBLK).astype(jnp.int32)
    branch = jax.random.randint(jax.random.fold_in(key, 4), (TOKENS, 1), 0, 4, dtype=jnp.int32)
    levels = jnp.arange(NB, dtype=jnp.int32)[None, :]
    node_index = jnp.where(levels == 0, 0, jnp.where(levels == 1, branch // 2, branch))
    return ordering[levels * 4 + node_index].astype(jnp.int32)


def with_ends(drawn, stream_key, smallest, largest):
    dims = drawn.shape
    index_at = [jax.random.randint(jax.random.fold_in(stream_key, axis), (), 0, dims[axis]) for axis in range(len(dims))]
    drawn = drawn.at[tuple(index_at)].set(smallest)
    longest = dims.index(max(dims))
    index_at[longest] = (index_at[longest] + 1) % dims[longest]
    return drawn.at[tuple(index_at)].set(largest)


def block_levels(rng, shape, shards, least, top_value):
    def one(dim, shards_of):
        steps = jax.random.uniform(jax.random.fold_in(jax.random.fold_in(rng, 6), dim), (shards_of,), jnp.float32, least / len(shards), top_value / len(shards))
        return jnp.repeat(jnp.exp(steps), shape[dim] // shards_of).reshape((-1,) + (1,) * (len(shape) - dim - 1))

    level = one(*shards[0])
    for cut in shards[1:]:
        level = level * one(*cut)
    return level


def routed_block(own_key, own, number, rows, count, top, bound, lean):
    sequence = jax.random.permutation(own_key, count)
    crowded, usual = shares(count, rows * top, bound, lean, True), shares(count, rows * top, bound, lean, False)
    places = jnp.arange(count)

    def named(sizes, turn):
        used = int((sizes > 0).sum())
        fixed = max(1, used // 4)
        passed = fixed + (places - fixed + turn * (used - fixed)) % max(1, count - fixed)
        return jnp.zeros((count,), jnp.int32).at[sequence[jnp.where(places < fixed, places, passed)]].set(jnp.asarray(sizes, jnp.int32))

    sizes = jnp.where(number % 4 == 0, named(crowded, number // 4), named(usual, number - number // 4 - 1))
    mixed = jax.random.permutation(jax.random.fold_in(own, 3), count)
    giver, receiver = mixed[0:count // 2 * 2:2], mixed[1:count // 2 * 2:2]
    room = jnp.minimum(sizes[giver] - 1, bound - sizes[receiver]) // 2
    room = jnp.where((giver == sequence[0]) | (receiver == sequence[0]) | (sizes[receiver] == 0), 0, jnp.maximum(room, 0))
    passed = jax.random.randint(jax.random.fold_in(own, 4), (count // 2,), 0, 1 << 20) % (room + 1)
    sizes = sizes.at[giver].add(-passed).at[receiver].add(passed)
    items = jnp.searchsorted(jnp.cumsum(sizes), jnp.arange(rows * top), side="right").astype(jnp.int32)
    grid = items.reshape(top, rows).T
    grid = grid[jax.random.permutation(jax.random.fold_in(own, 1), rows)]
    turn = jax.random.randint(jax.random.fold_in(own, 2), (rows, 1), 0, top)
    return jnp.take_along_axis(grid, (jnp.arange(top)[None, :] + turn) % top, axis=1)


def shares(amount, total, most, skew, full):
    loads = [(1 << 20) // math.isqrt(rank ** skew) + 1 for rank in range(1, amount + 1)]
    largest = most if full else min(most, max(-(-total // amount), total * loads[0] // sum(loads)))
    least = 1 if total - largest >= amount - 1 else 0
    given, rest = [largest] + [least] * (amount - 1), total - largest - least * (amount - 1)
    while rest > 0:
        movable = [i for i in range(1, amount) if given[i] < largest] or [i for i in range(1, amount) if given[i] < most]
        pool, left = sum([loads[i] for i in movable]), rest
        for i in movable:
            more = min(most - given[i], max(1, left * loads[i] // pool), rest)
            given[i] = given[i] + more
            rest = rest - more
    return np.array(given)


def normal_values(own_key, extent, spread, bound, split=(), kind=jnp.bfloat16):
    values = jax.random.normal(own_key, extent, jnp.float32) * spread
    if len(split) > 0:
        values = block_levels(own_key, extent, split, -0.22, 0.18) * values
    return jnp.clip(values, min=-bound, max=bound).astype(kind)


def setup_inputs(seed: int = 0) -> dict:
    seeds = jax.random.split(jax.random.key(seed), 16)
    hidden_in = normal_values(seeds[0], (TOKENS, D), 1.0, 6.0, ((0, 32),))
    query = draw_query(jax.random.fold_in(seeds[15], 71), 0)
    prefix_pool = draw_prefix_pool(jax.random.fold_in(seeds[15], 71), 0)
    suffix_cache = draw_suffix_cache(jax.random.fold_in(seeds[15], 71), 0)
    block_list = draw_block_list(jax.random.fold_in(seeds[15], 71), 0)
    prefix_count = with_ends(jax.random.randint(seeds[5], (TOKENS,), 1, NB + 1), jax.random.fold_in(seeds[5], 1), 1, NB).astype(jnp.int32)
    suffix_count = with_ends(jax.random.randint(seeds[6], (TOKENS,), 1, SUFFIX + 1), jax.random.fold_in(seeds[6], 1), 1, SUFFIX).astype(jnp.int32)
    value_up = normal_values(seeds[7], (HEADS, LAT, VH), LAT ** -0.5, 0.25, ((0, 8),))
    out_proj = normal_values(seeds[8], (HEADS * VH, D), VH ** -0.5, 0.5, ((0, 8),))
    norm_gain = jnp.clip(1.0 + 0.1 * jax.random.normal(seeds[9], (D,), jnp.float32), 0.5, 1.5).astype(jnp.bfloat16)
    expert_ids_keys = jax.random.split(jax.random.fold_in(seeds[10], 1), TOKENS // REQ_DEV)
    expert_ids_turns = jax.random.permutation(jax.random.fold_in(seeds[10], 3), TOKENS // REQ_DEV)
    expert_ids = jax.vmap(lambda own, number: routed_block(jax.random.fold_in(seeds[10], 2), own, number, REQ_DEV, EXPERTS, TOPK, CAP, 2))(expert_ids_keys, expert_ids_turns).reshape((TOKENS, TOPK))
    gate_weights = jnp.clip(jnp.exp(math.log(1.0) - 2.9996462 * jax.random.uniform(seeds[11], (TOKENS, TOPK), jnp.float32) ** block_levels(seeds[11], (TOKENS, TOPK), ((0, 32),), -0.2, 0.2)), 0.049804688, 1.0).astype(jnp.bfloat16)
    gate_proj = normal_values(seeds[12], (EXPERTS, D, FF), D ** -0.5, 0.078125, ((0, 8), (2, 4)))
    up_proj = normal_values(seeds[13], (EXPERTS, D, FF), D ** -0.5, 0.078125, ((0, 8), (2, 4)))
    down_proj = normal_values(seeds[14], (EXPERTS, FF, D), FF ** -0.5, 0.15625, ((0, 8), (1, 4)))
    return dict(hidden_in=hidden_in, query=query, prefix_pool=prefix_pool, suffix_cache=suffix_cache, block_list=block_list, prefix_count=prefix_count, suffix_count=suffix_count, value_up=value_up, out_proj=out_proj, norm_gain=norm_gain, expert_ids=expert_ids, gate_weights=gate_weights, gate_proj=gate_proj, up_proj=up_proj, down_proj=down_proj)


NEG_FILL = -1e+30
SCORE_SCALE = 192.0 ** (-0.5)
NORM_EPS = 1e-06

def slot_table(expert_rows, expert_total):
    matches = (expert_rows[..., None] == jnp.arange(expert_total, dtype=jnp.int32)).astype(jnp.int32)
    row_load = lax.optimization_barrier(jnp.sum(matches, axis=-2))
    earlier = jnp.cumsum(row_load, axis=-2) - row_load
    return lax.optimization_barrier(jnp.sum(matches * earlier[..., None, :], axis=-1))

def reference(hidden_in, query, prefix_pool, suffix_cache, block_list, prefix_count, suffix_count, value_up, out_proj, norm_gain, expert_ids, gate_weights, gate_proj, up_proj, down_proj):
    groups = TOKENS // REQ_DEV
    pool_rows = prefix_pool.reshape(NBLK, BLOCK, KDIM)
    grouped = (query.reshape(groups, REQ_DEV, HEADS, KDIM), suffix_cache.reshape(groups, REQ_DEV, SUFFIX, KDIM), block_list.reshape(groups, REQ_DEV, NB), prefix_count.reshape(groups, REQ_DEV), suffix_count.reshape(groups, REQ_DEV))

    def attend(member):
        queries, own_keys, block_rows, counts, own_counts = member
        prefix_keys = pool_rows[block_rows].reshape(REQ_DEV, NB * BLOCK, KDIM)
        all_keys = jnp.concatenate([prefix_keys, own_keys], axis=1).astype(jnp.float32)
        prefix_live = (jnp.arange(NB * BLOCK, dtype=jnp.int32) // BLOCK)[None, :] < counts[:, None]
        own_live = jnp.arange(SUFFIX, dtype=jnp.int32)[None, :] < own_counts[:, None]
        live_mask = jnp.concatenate([prefix_live, own_live], axis=1)[:, None, :]
        scores = jnp.einsum('rhk,rnk->rhn', queries.astype(jnp.float32), all_keys) * SCORE_SCALE
        scores = jnp.where(live_mask, scores, NEG_FILL)
        row_max = lax.optimization_barrier(jnp.max(scores, axis=-1, keepdims=True))
        weights = jnp.where(live_mask, jnp.exp(scores - row_max), 0.0)
        denominator = lax.optimization_barrier(jnp.sum(weights, axis=-1))
        rounded = lax.optimization_barrier(weights.astype(jnp.bfloat16)).astype(jnp.float32)
        numerator = jnp.einsum('rhn,rnl->rhl', rounded, all_keys[:, :, :LAT])
        return (numerator / denominator[..., None]).astype(jnp.bfloat16)
    context = lax.map(attend, grouped).reshape(TOKENS, HEADS, LAT)
    head_values = jnp.einsum('thl,hlv->thv', context.astype(jnp.float32), value_up.astype(jnp.float32)).astype(jnp.bfloat16)
    attended = jnp.dot(head_values.reshape(TOKENS, HEADS * VH), out_proj, preferred_element_type=jnp.float32)
    residual_out = hidden_in.astype(jnp.float32) + attended
    widened = residual_out
    scale_rows = lax.rsqrt(lax.optimization_barrier(jnp.mean(widened * widened, axis=-1, keepdims=True)) + NORM_EPS)
    normed = (widened * scale_rows * norm_gain.astype(jnp.float32)).astype(jnp.bfloat16)
    routed = expert_ids.reshape(groups, REQ_DEV, TOPK)
    slots = slot_table(routed, EXPERTS)
    token_rows = normed.reshape(groups, REQ_DEV, D).astype(jnp.float32)
    gates = gate_weights.reshape(groups, REQ_DEV, TOPK).astype(jnp.float32)
    slot_match = slots[..., None] == jnp.arange(CAP, dtype=jnp.int32)

    def per_expert(running, weights_of):
        gate_w, up_w, down_w, expert_index = weights_of
        chosen = (routed == expert_index)[..., None] & slot_match
        select = jnp.any(chosen, axis=2).astype(jnp.float32)
        combine = lax.optimization_barrier(jnp.sum(jnp.where(chosen, gates[..., None], 0.0), axis=2))
        rows_in = jnp.einsum('dtc,dtm->dcm', select, token_rows).astype(jnp.bfloat16).reshape(groups * CAP, D)
        gate_part = jnp.dot(rows_in, gate_w, preferred_element_type=jnp.float32)
        up_part = jnp.dot(rows_in, up_w, preferred_element_type=jnp.float32)
        hidden = (jax.nn.silu(gate_part) * up_part).astype(jnp.bfloat16)
        pieces = jnp.einsum('mgk,gkd->mgd', hidden.reshape(groups * CAP, N_DP, FF_GROUP).astype(jnp.float32), down_w.reshape(N_DP, FF_GROUP, D).astype(jnp.float32))
        pieces = lax.optimization_barrier(pieces.astype(jnp.bfloat16)).astype(jnp.float32)
        outputs = lax.optimization_barrier(jnp.sum(pieces, axis=1)).reshape(groups, CAP, D)
        return (running + jnp.einsum('dtc,dcm->dtm', combine, outputs), None)
    initial = jnp.zeros((groups, REQ_DEV, D), jnp.float32)
    moe_sum, unused = lax.scan(per_expert, initial, (gate_proj, up_proj, down_proj, jnp.arange(EXPERTS, dtype=jnp.int32)))
    return (residual_out, moe_sum.reshape(TOKENS, D))
```

```python
import jax
import jax.numpy as jnp
from jax import lax
from jax.sharding import PartitionSpec as P

HEADS = 64
LAT = 512
TOPK = 6
BLOCK = 64
SUFFIX = 128
KDIM = 576


NEG_FILL = -1e30
SCORE_SCALE = 192.0 ** (-0.5)
NORM_EPS = 1e-06
LANES = 128


def swap(value, axis, mask):
    size = lax.axis_size(axis)
    return lax.ppermute(value, axis, [(i, i ^ mask) for i in range(size)])


def rounded(value):
    return lax.reduce_precision(value, 8, 7)


def dot(a, b, dims):
    return lax.dot_general(a, b, (dims, ((), ())), preferred_element_type=jnp.float32)


def own_partial(queries, own_keys, own_live):
    scores = (
        jnp.einsum("rhk,rnk->rhn", queries, own_keys, preferred_element_type=jnp.float32)
        * SCORE_SCALE
    )
    live_keys = own_live[:, None, :]
    scores = jnp.where(live_keys, scores, NEG_FILL)
    row_max = rounded(jnp.max(scores, axis=-1))
    weights = jnp.where(live_keys, jnp.exp(scores - row_max[..., None]), 0.0)
    numerator = jnp.einsum(
        "rhn,rnl->rhl",
        weights.astype(jnp.bfloat16),
        own_keys[:, :, :LAT],
        preferred_element_type=jnp.float32,
    )
    return (row_max, jnp.sum(weights, axis=-1), numerator)


def split_heads(value, members, place):
    rows, heads, width = value.shape
    groups = value.reshape(rows, members, heads // members, width)
    return [
        lax.dynamic_index_in_dim(groups, place ^ j, 1, keepdims=False) for j in range(members)
    ]


def to_head_owners(value, members, place):
    groups = split_heads(value, members, place)
    chips = members // 2
    mine = jnp.stack(groups[0::2])
    other = swap(jnp.stack(groups[1::2]), "expert", 1)
    both = jnp.stack([mine, other], axis=1)
    return jnp.concatenate(
        [both[:1]] + [swap(both[k], "expert", 2 * k)[None] for k in range(1, chips)]
    )


def sum_over_heads(partial, members):
    chips = members // 2
    away = swap(partial[:, 1].astype(jnp.bfloat16), "expert", 1)
    held = partial[:, 0] + away.astype(jnp.float32)
    total = held[0]
    sent = held.astype(jnp.bfloat16)
    for k in range(1, chips):
        total = total + swap(sent[k], "expert", 2 * k).astype(jnp.float32)
    return total


def spread(rows, members, holders):
    by_z = jnp.stack([rows] + [swap(rows, "dp", q) for q in range(1, holders)])
    by_chip = jnp.stack([by_z] + [swap(by_z, "expert", 2 * k) for k in range(1, members // 2)])
    return jnp.stack([by_chip, swap(by_chip, "expert", 1)])


def gather_sums(partial, members, holders):
    held = partial[0].astype(jnp.float32) + swap(partial[1], "expert", 1).astype(jnp.float32)
    sent = held.astype(jnp.bfloat16)
    total = held[0]
    for k in range(1, members // 2):
        total = total + swap(sent[k], "expert", 2 * k).astype(jnp.float32)
    sent = total.astype(jnp.bfloat16)
    result = total[0]
    for q in range(1, holders):
        result = result + swap(sent[q], "dp", q).astype(jnp.float32)
    return result


def per_device(
    hidden_in,
    query,
    prefix_pool,
    suffix_cache,
    block_list,
    prefix_count,
    suffix_count,
    value_up,
    out_proj,
    norm_gain,
    expert_ids,
    gate_weights,
    gate_proj,
    up_proj,
    down_proj,
):
    bf16 = jnp.bfloat16
    row_count, width = hidden_in.shape
    members = lax.axis_size("expert")
    holders = lax.axis_size("dp")
    chips = members // 2
    place = lax.axis_index("expert")
    shard = lax.axis_index("dp")
    shard_blocks = prefix_pool.shape[0]
    total_blocks = shard_blocks * holders

    shard_rows = shard_blocks * BLOCK
    row_block = shard * shard_blocks + jnp.arange(shard_rows, dtype=jnp.int32) // BLOCK
    one_hot = (row_block[:, None] == jnp.arange(total_blocks, dtype=jnp.int32)).astype(bf16)
    own_pool = jnp.concatenate([prefix_pool.reshape(shard_rows, KDIM), one_hot], axis=1)
    slice_rows = shard_rows // members
    piece = lax.dynamic_slice_in_dim(own_pool, place * slice_rows, slice_rows, 0)
    arrived = [swap(piece, "dp", q) for q in range(1, holders)]

    queries = query.reshape(row_count, HEADS, KDIM)
    own_keys = suffix_cache.reshape(row_count, SUFFIX, KDIM)
    own_live = jnp.arange(SUFFIX, dtype=jnp.int32)[None, :] < suffix_count[:, None]
    own_max, own_sum, own_num = own_partial(queries, own_keys, own_live)
    sum_high = rounded(own_sum)
    stats = jnp.stack([own_max, sum_high, own_sum - sum_high], axis=-1).astype(bf16)
    in_prefix = jnp.arange(block_list.shape[1], dtype=jnp.int32)[None, :] < prefix_count[:, None]
    member = jnp.any(
        (block_list[:, :, None] == jnp.arange(total_blocks, dtype=jnp.int32))
        & in_prefix[:, :, None],
        axis=1,
    )
    bias = jnp.where(member, 0.0, NEG_FILL).astype(bf16)
    bias = jnp.broadcast_to(bias[:, None, :], (row_count, HEADS, total_blocks))
    payload = jnp.concatenate(
        [
            queries,
            bias,
            own_num.astype(bf16),
            jnp.pad(stats, ((0, 0), (0, 0), (0, LANES - stats.shape[-1]))),
        ],
        axis=-1,
    )
    held = to_head_owners(payload, members, place)
    key_width = KDIM + total_blocks
    flat = held.reshape(-1, held.shape[-1])
    head_queries = flat[:, :key_width]
    own_num = flat[:, key_width : key_width + LAT].astype(jnp.float32)
    stats = flat[:, key_width + LAT :].astype(jnp.float32)
    own_max = stats[:, 0:1]
    own_sum = stats[:, 1:2] + stats[:, 2:3]

    chunks = [own_pool]
    for block in arrived:
        mine = jnp.concatenate([block] + [swap(block, "expert", 2 * k) for k in range(1, chips)])
        chunks.append(mine)
        chunks.append(swap(mine, "expert", 1))
    scores = [dot(head_queries, keys, ((1,), (1,))) * SCORE_SCALE for keys in chunks]
    new_max = own_max
    for part in scores:
        new_max = jnp.maximum(new_max, jnp.max(part, axis=-1, keepdims=True))
    rescale = jnp.exp(own_max - new_max)
    numerator = own_num * rescale
    denominator = own_sum * rescale
    for part, keys in zip(scores, chunks):
        weights = jnp.exp(part - new_max)
        denominator = denominator + jnp.sum(weights, axis=-1, keepdims=True)
        numerator = numerator + dot(weights.astype(bf16), keys[:, :LAT], ((1,), (0,)))
    context = (numerator / denominator).astype(bf16)

    group_heads = HEADS // members
    context = context.reshape(-1, group_heads, LAT)
    head_values = jnp.einsum(
        "thl,hlv->thv", context, value_up, preferred_element_type=jnp.float32
    ).astype(bf16)
    value_rows = head_values.reshape(head_values.shape[0], -1)
    partial = jnp.dot(value_rows, out_proj, preferred_element_type=jnp.float32)
    attended = sum_over_heads(partial.reshape(chips, 2, row_count, width), members)
    residual_out = hidden_in.astype(jnp.float32) + attended
    scale_rows = lax.rsqrt(jnp.mean(residual_out * residual_out, axis=-1, keepdims=True) + NORM_EPS)
    normed = (residual_out * scale_rows * norm_gain.astype(jnp.float32)).astype(bf16)

    expert_total = gate_proj.shape[0] * members
    chosen = expert_ids[:, :, None] == jnp.arange(LANES, dtype=jnp.int32)
    gates = jnp.sum(jnp.where(chosen, gate_weights[:, :, None], 0.0), axis=1).astype(bf16)
    rows = spread(jnp.concatenate([normed, gates], axis=1), members, holders)
    flat = rows.reshape(-1, width + LANES)
    tokens = flat[:, :width]
    gate = lax.dynamic_slice_in_dim(flat[:, width:], place, 1, 1).astype(jnp.float32)
    gate_part = jnp.dot(tokens, gate_proj[0], preferred_element_type=jnp.float32)
    up_part = jnp.dot(tokens, up_proj[0], preferred_element_type=jnp.float32)
    hidden = (jax.nn.silu(gate_part) * up_part).astype(bf16)
    result = jnp.dot(hidden, down_proj[0], preferred_element_type=jnp.float32) * gate
    result = result.astype(bf16).reshape(2, chips, holders, row_count, width)
    moe_sum = gather_sums(result, members, holders)
    return (residual_out, moe_sum)


def solution(mesh):
    in_specs = (
        P(("dp", "expert"), None),
        P(("dp", "expert"), None),
        P("dp", None),
        P(("dp", "expert"), None),
        P(("dp", "expert"), None),
        P(("dp", "expert")),
        P(("dp", "expert")),
        P("expert", None, None),
        P("expert", None),
        P(),
        P(("dp", "expert"), None),
        P(("dp", "expert"), None),
        P("expert", None, "dp"),
        P("expert", None, "dp"),
        P("expert", "dp", None),
    )
    out_specs = (P(("dp", "expert"), None), P(("dp", "expert"), None))
    return jax.shard_map(
        per_device, mesh=mesh, in_specs=in_specs, out_specs=out_specs, check_vma=False
    )
```

```python
import functools

import jax
import jax.numpy as jnp
from jax import lax
from jax.experimental import pallas as pl
from jax.experimental.pallas import tpu as pltpu
from jax.sharding import PartitionSpec as P

HEADS = 64
LAT = 512
TOPK = 6
BLOCK = 64
SUFFIX = 128
KDIM = 576


NEG_FILL = -1e30
SCORE_SCALE = 192.0 ** (-0.5)
NORM_EPS = 1e-06
LANES = 128


def swap(value, axis, mask):
    size = lax.axis_size(axis)
    return lax.ppermute(value, axis, [(i, i ^ mask) for i in range(size)])


def rounded(value):
    return lax.reduce_precision(value, 8, 7)


def dot(a, b, dims):
    return lax.dot_general(a, b, (dims, ((), ())), preferred_element_type=jnp.float32)


def vmem_call(kernel, out_shape, operands, flops, scalars=0):
    specs = [pl.BlockSpec(memory_space=pltpu.SMEM)] * scalars
    specs += [pl.BlockSpec(memory_space=pltpu.VMEM)] * (len(operands) - scalars)
    size = sum(o.size * o.dtype.itemsize for o in operands)
    return pl.pallas_call(
        kernel,
        out_shape=out_shape,
        in_specs=specs,
        out_specs=jax.tree.map(lambda _: pl.BlockSpec(memory_space=pltpu.VMEM), out_shape),
        cost_estimate=pl.CostEstimate(flops=flops, bytes_accessed=size, transcendentals=0),
        compiler_params=pltpu.CompilerParams(vmem_limit_bytes=48 * 1024 * 1024),
    )(*operands)


def suffix_kernel(count_ref, query_ref, keys_ref, out_ref):
    for r in range(query_ref.shape[0]):
        keys = keys_ref[r]
        scores = dot(query_ref[r], keys, ((1,), (1,))) * SCORE_SCALE
        live = lax.broadcasted_iota(jnp.int32, scores.shape, 1) < count_ref[r]
        scores = jnp.where(live, scores, NEG_FILL)
        top = jnp.max(scores, axis=-1, keepdims=True).astype(jnp.bfloat16).astype(jnp.float32)
        weights = jnp.where(live, jnp.exp(scores - top), 0.0)
        total = jnp.sum(weights, axis=-1, keepdims=True)
        high = total.astype(jnp.bfloat16).astype(jnp.float32)
        numerator = dot(weights.astype(jnp.bfloat16), keys[:, :LAT], ((1,), (0,)))
        lane = lax.broadcasted_iota(jnp.int32, (scores.shape[0], LANES), 1)
        stats = jnp.where(lane == 0, top, jnp.where(lane == 1, high, total - high))
        out_ref[r, :, :LAT] = numerator.astype(jnp.bfloat16)
        out_ref[r, :, LAT:] = stats.astype(jnp.bfloat16)


PAIR = 2 * KDIM
WIDE = KDIM + 64


def pair_keys(chunks, spot):
    blocks = chunks[0].shape[0]
    lane = lax.broadcasted_iota(jnp.int32, (blocks, LANES), 1)
    block = lax.broadcasted_iota(jnp.int32, (blocks, LANES), 0)
    first = (lane < 64).astype(jnp.float32).astype(jnp.bfloat16)
    last = (lane >= 64).astype(jnp.float32).astype(jnp.bfloat16)
    hot_even = (lane == 64 + spot + block).astype(jnp.float32).astype(jnp.bfloat16)
    hot_odd = (lane == spot + block).astype(jnp.float32).astype(jnp.bfloat16)
    even, odd = [], []
    for ref in chunks:
        for at in range(0, ref.shape[1], PAIR):
            middle = ref[:, at + LAT : at + LAT + LANES]
            even.append(
                jnp.concatenate([ref[:, at : at + LAT], middle * first + hot_even], axis=1)
            )
            odd.append(
                jnp.concatenate(
                    [middle * last + hot_odd, ref[:, at + LAT + LANES : at + PAIR]], axis=1
                )
            )
    return jnp.concatenate(even, axis=0), jnp.concatenate(odd, axis=0)


def advance(query_even, query_odd, even, odd, state):
    score_even = dot(query_even, even, ((1,), (1,))) * SCORE_SCALE
    score_odd = dot(query_odd, odd, ((1,), (1,))) * SCORE_SCALE
    top = jnp.maximum(
        jnp.max(score_even, axis=-1, keepdims=True), jnp.max(score_odd, axis=-1, keepdims=True)
    )
    if state is not None:
        top = jnp.maximum(top, state[0])
    weight_even = jnp.exp(score_even - top)
    weight_odd = jnp.exp(score_odd - top)
    total = jnp.sum(weight_even, axis=-1, keepdims=True)
    total = total + jnp.sum(weight_odd, axis=-1, keepdims=True)
    sum_even = dot(weight_even.astype(jnp.bfloat16), even[:, :LAT], ((1,), (0,)))
    sum_odd = dot(weight_odd.astype(jnp.bfloat16), odd, ((1,), (0,)))
    if state is not None:
        keep = jnp.exp(state[0] - top)
        total = total + state[1] * keep
        sum_even = sum_even + state[2] * keep
        sum_odd = sum_odd + state[3] * keep
    return top, total, sum_even, sum_odd


def prefix_kernel(count, spots, has_state, *refs):
    query_even, query_odd = refs[0][...], refs[1][...]
    refs = refs[2:]
    state = None
    if has_state:
        state = (refs[0][:, :1], refs[1][:, :1], refs[2][...], refs[3][...])
        refs = refs[4:]
    for spot in spots:
        even, odd = pair_keys(refs[:count], spot)
        refs = refs[count:]
        state = advance(query_even, query_odd, even, odd, state)
    top_ref, total_ref, even_ref, odd_ref = refs
    top_ref[...] = jnp.broadcast_to(state[0], top_ref.shape)
    total_ref[...] = jnp.broadcast_to(state[1], total_ref.shape)
    even_ref[...] = state[2]
    odd_ref[...] = state[3]


def prefix_step(queries, sources, spots, state):
    rows = queries[0].shape[0]
    count = len(sources[0])
    chunks = [c for source in sources for c in source]
    operands = list(queries) + list(state or ()) + chunks
    f32 = jnp.float32
    out_shape = (
        jax.ShapeDtypeStruct((rows, LANES), f32),
        jax.ShapeDtypeStruct((rows, LANES), f32),
        jax.ShapeDtypeStruct((rows, LAT), f32),
        jax.ShapeDtypeStruct((rows, WIDE), f32),
    )
    flops = sum(c.size for c in chunks) * rows * 4
    kernel = functools.partial(prefix_kernel, count, tuple(spots), state is not None)
    return vmem_call(kernel, out_shape, operands, flops)


def finish_kernel(top_ref, total_ref, even_ref, odd_ref, own_ref, value_ref, out_ref):
    heads = value_ref.shape[0]
    rows = top_ref.shape[0] // heads
    for h in range(heads):
        at = pl.ds(h * rows, rows)
        stats = own_ref[at, LAT:].astype(jnp.float32)
        own_top = stats[:, 0:1]
        own_total = stats[:, 1:2] + stats[:, 2:3]
        top = jnp.maximum(top_ref[at, :1], own_top)
        keep = jnp.exp(top_ref[at, :1] - top)
        own_keep = jnp.exp(own_top - top)
        numerator = (even_ref[at, :] + odd_ref[at, 64 : 64 + LAT]) * keep
        numerator = numerator + own_ref[at, :LAT].astype(jnp.float32) * own_keep
        total = total_ref[at, :1] * keep + own_total * own_keep
        context = (numerator / total).astype(jnp.bfloat16)
        out_ref[:, h * value_ref.shape[2] : (h + 1) * value_ref.shape[2]] = dot(
            context, value_ref[h], ((1,), (0,))
        ).astype(jnp.bfloat16)


def to_head_owners(groups, members):
    chips = members // 2
    mine = jnp.stack(groups[0::2])
    other = swap(jnp.stack(groups[1::2]), "expert", 1)
    both = jnp.stack([mine, other], axis=1)
    return jnp.stack([both[0]] + [swap(both[k], "expert", 2 * k) for k in range(1, chips)])


def sum_over_heads(partial, members):
    chips = members // 2
    away = swap(partial[:, 1].astype(jnp.bfloat16), "expert", 1)
    held = partial[:, 0] + away.astype(jnp.float32)
    total = held[0]
    sent = held.astype(jnp.bfloat16)
    for k in range(1, chips):
        total = total + swap(sent[k], "expert", 2 * k).astype(jnp.float32)
    return total


def spread(rows, members, holders):
    by_z = jnp.stack([rows] + [swap(rows, "dp", q) for q in range(1, holders)])
    by_chip = jnp.stack([by_z] + [swap(by_z, "expert", 2 * k) for k in range(1, members // 2)])
    return jnp.stack([by_chip, swap(by_chip, "expert", 1)])


def gather_sums(partial, members, holders):
    held = partial[0].astype(jnp.float32) + swap(partial[1], "expert", 1).astype(jnp.float32)
    sent = held.astype(jnp.bfloat16)
    total = held[0]
    for k in range(1, members // 2):
        total = total + swap(sent[k], "expert", 2 * k).astype(jnp.float32)
    sent = total.astype(jnp.bfloat16)
    result = total[0]
    for q in range(1, holders):
        result = result + swap(sent[q], "dp", q).astype(jnp.float32)
    return result


def per_device(
    hidden_in,
    query,
    prefix_pool,
    suffix_cache,
    block_list,
    prefix_count,
    suffix_count,
    value_up,
    out_proj,
    norm_gain,
    expert_ids,
    gate_weights,
    gate_proj,
    up_proj,
    down_proj,
):
    bf16 = jnp.bfloat16
    row_count, width = hidden_in.shape
    members = lax.axis_size("expert")
    holders = lax.axis_size("dp")
    chips = members // 2
    place = lax.axis_index("expert")
    shard = lax.axis_index("dp")
    shard_blocks = prefix_pool.shape[0]
    total_blocks = shard_blocks * holders

    piece_width = prefix_pool.shape[1] // members
    piece = lax.dynamic_slice_in_dim(prefix_pool, place * piece_width, piece_width, 1)
    arrived = [swap(piece, "dp", q) for q in range(1, holders)]

    in_prefix = jnp.arange(block_list.shape[1], dtype=jnp.int32)[None, :] < prefix_count[:, None]
    slots = jnp.arange(total_blocks, dtype=jnp.int32)
    ids = (shard ^ (slots // shard_blocks)) * shard_blocks + slots % shard_blocks
    member = jnp.any((block_list[:, :, None] == ids) & in_prefix[:, :, None], axis=1)
    bias = jnp.where(member, 0.0, NEG_FILL).astype(bf16)
    bias = jnp.pad(bias, ((0, 0), (0, LANES - total_blocks)))
    group_heads = HEADS // members
    group_width = group_heads * KDIM
    groups = [
        jnp.concatenate(
            [
                lax.dynamic_slice_in_dim(query, (place ^ j) * group_width, group_width, 1),
                bias,
            ],
            axis=1,
        )
        for j in range(members)
    ]
    held = to_head_owners(groups, members).reshape(-1, group_width + LANES)
    head_queries = held[:, :group_width].reshape(-1, group_heads, KDIM)
    head_queries = head_queries.transpose(1, 0, 2).reshape(-1, KDIM)
    head_bias = jnp.tile(held[:, group_width:], (group_heads, 1))
    variants = []
    for at in range(0, total_blocks, 64):
        part = head_bias[:, at : at + 64]
        variants.append(
            (
                jnp.concatenate([head_queries, part], axis=1),
                jnp.concatenate([part, head_queries], axis=1),
            )
        )

    queries = query.reshape(row_count, HEADS, KDIM)
    own_keys = suffix_cache.reshape(row_count, SUFFIX, KDIM)
    own = vmem_call(
        suffix_kernel,
        jax.ShapeDtypeStruct((row_count, HEADS, LAT + LANES), bf16),
        [suffix_count, queries, own_keys],
        4 * row_count * HEADS * SUFFIX * KDIM,
        scalars=1,
    )
    own_groups = own.reshape(row_count, members, group_heads, LAT + LANES)
    own = to_head_owners(
        [
            lax.dynamic_index_in_dim(own_groups, place ^ j, 1, keepdims=False)
            for j in range(members)
        ],
        members,
    )
    own = own.reshape(-1, group_heads, LAT + LANES).transpose(1, 0, 2)
    own = own.reshape(-1, LAT + LANES)

    state = prefix_step(variants[0], [[prefix_pool]], [0], None)
    for q in range(1, holders):
        mine = [arrived[q - 1]]
        mine += [swap(mine[0], "expert", 2 * k) for k in range(1, chips)]
        chunks = mine + [swap(block, "expert", 1) for block in mine]
        spot = q * shard_blocks
        state = prefix_step(variants[spot // 64], [chunks], [spot % 64], state)
    value_rows = vmem_call(
        finish_kernel,
        jax.ShapeDtypeStruct((state[0].shape[0] // group_heads, group_heads * 128), bf16),
        list(state) + [own, value_up],
        2 * state[2].size * 128,
    )
    partial = jnp.dot(value_rows, out_proj, preferred_element_type=jnp.float32)
    attended = sum_over_heads(partial.reshape(chips, 2, row_count, width), members)
    residual_out = hidden_in.astype(jnp.float32) + attended
    scale_rows = lax.rsqrt(jnp.mean(residual_out * residual_out, axis=-1, keepdims=True) + NORM_EPS)
    normed = (residual_out * scale_rows * norm_gain.astype(jnp.float32)).astype(bf16)

    expert_total = gate_proj.shape[0] * members
    chosen = expert_ids[:, :, None] == jnp.arange(LANES, dtype=jnp.int32)
    gates = jnp.sum(jnp.where(chosen, gate_weights[:, :, None], 0.0), axis=1).astype(bf16)
    rows = spread(jnp.concatenate([normed, gates], axis=1), members, holders)
    flat = rows.reshape(-1, width + LANES)
    tokens = flat[:, :width]
    gate = lax.dynamic_slice_in_dim(flat[:, width:], place, 1, 1).astype(jnp.float32)
    gate_part = jnp.dot(tokens, gate_proj[0], preferred_element_type=jnp.float32)
    up_part = jnp.dot(tokens, up_proj[0], preferred_element_type=jnp.float32)
    hidden = (jax.nn.silu(gate_part) * up_part).astype(bf16)
    result = jnp.dot(hidden, down_proj[0], preferred_element_type=jnp.float32) * gate
    result = result.astype(bf16).reshape(2, chips, holders, row_count, width)
    moe_sum = gather_sums(result, members, holders)
    return (residual_out, moe_sum)


def solution(mesh):
    in_specs = (
        P(("dp", "expert"), None),
        P(("dp", "expert"), None),
        P("dp", None),
        P(("dp", "expert"), None),
        P(("dp", "expert"), None),
        P(("dp", "expert")),
        P(("dp", "expert")),
        P("expert", None, None),
        P("expert", None),
        P(),
        P(("dp", "expert"), None),
        P(("dp", "expert"), None),
        P("expert", None, "dp"),
        P("expert", None, "dp"),
        P("expert", "dp", None),
    )
    out_specs = (P(("dp", "expert"), None), P(("dp", "expert"), None))
    return jax.shard_map(
        per_device, mesh=mesh, in_specs=in_specs, out_specs=out_specs, check_vma=False
    )
```

```python
import functools

import jax
import jax.numpy as jnp
import numpy as np
from jax import lax
from jax.experimental import pallas as pl
from jax.experimental.pallas import tpu as pltpu
from jax.sharding import PartitionSpec as P

HEADS = 64
LAT = 512
TOPK = 6
BLOCK = 64
SUFFIX = 128
KDIM = 576


NEG_FILL = -1e30
SCORE_SCALE = 192.0 ** (-0.5)
NORM_EPS = 1e-06
LANES = 128
PAIR = 2 * KDIM
WIDE = KDIM + 64


def swap(value, axis, mask):
    size = lax.axis_size(axis)
    return lax.ppermute(value, axis, [(i, i ^ mask) for i in range(size)])


def dot(a, b, dims):
    return lax.dot_general(a, b, (dims, ((), ())), preferred_element_type=jnp.float32)


def vmem_call(kernel, out_shape, operands, flops, scalars=0, scratch=(), away=(), grant=16):
    specs = [pl.BlockSpec(memory_space=pltpu.SMEM)] * scalars
    specs += [pl.BlockSpec(memory_space=pltpu.VMEM)] * (len(operands) - scalars)
    specs += [pl.BlockSpec(memory_space=pl.ANY)] * len(away)
    size = sum(o.size * o.dtype.itemsize for o in operands)
    return pl.pallas_call(
        kernel,
        out_shape=out_shape,
        in_specs=specs,
        out_specs=jax.tree.map(lambda _: pl.BlockSpec(memory_space=pltpu.VMEM), out_shape),
        scratch_shapes=list(scratch),
        cost_estimate=pl.CostEstimate(flops=flops, bytes_accessed=size, transcendentals=0),
        compiler_params=pltpu.CompilerParams(vmem_limit_bytes=grant * 1024 * 1024),
    )(*operands, *away)


def suffix_kernel(pos, query_ref, keys_ref, count_hbm, mine_ref, other_ref, rows, count, sem):
    copy = pltpu.make_async_copy(count_hbm, count, sem)
    copy.start()
    place = pos[0]
    requests, heads, _ = query_ref.shape
    chips, group_rows, width = mine_ref.shape
    group = group_rows // requests
    members = heads // group
    all_scores = [
        dot(query_ref[r], keys_ref[r], ((1,), (1,))) * SCORE_SCALE for r in range(requests)
    ]
    copy.wait()
    for r in range(requests):
        scores = all_scores[r]
        live = lax.broadcasted_iota(jnp.int32, scores.shape, 1) < count[r]
        scores = jnp.where(live, scores, NEG_FILL)
        top = jnp.max(scores, axis=-1, keepdims=True).astype(jnp.bfloat16).astype(jnp.float32)
        weights = jnp.where(live, jnp.exp(scores - top), 0.0)
        total = jnp.sum(weights, axis=-1, keepdims=True)
        high = total.astype(jnp.bfloat16).astype(jnp.float32)
        numerator = dot(weights.astype(jnp.bfloat16), keys_ref[r, :, :LAT], ((1,), (0,)))
        lane = lax.broadcasted_iota(jnp.int32, (heads, LANES), 1)
        stats = jnp.where(lane == 0, top, jnp.where(lane == 1, high, total - high))
        full = jnp.concatenate([numerator, stats], axis=1)
        for g in range(members):
            rows[r, g] = full[g * group : (g + 1) * group]
    for j in range(members):
        taken = [rows[r, place ^ j] for r in range(requests)]
        out_ref = other_ref if j % 2 else mine_ref
        out_ref[j // 2] = jnp.concatenate(taken, axis=0).astype(jnp.bfloat16)


def join_kernel(mine_ref, other_ref, piece_ref, *outs):
    width = mine_ref.shape[2]
    blocks = piece_ref.shape[0]
    for k, out_ref in enumerate(outs):
        both = [mine_ref[k].astype(jnp.float32), other_ref[k].astype(jnp.float32)]
        out_ref[:, :width] = jnp.concatenate(both, axis=0).astype(jnp.bfloat16)
        for i in range(piece_ref.shape[1] // PAIR):
            out_ref[i * blocks : (i + 1) * blocks, width:] = piece_ref[:, i * PAIR : (i + 1) * PAIR]


def lane_pairs(refs, row):
    return [(ref, row, at) for ref in refs for at in range(0, ref.shape[1], PAIR)]


def stacked_pairs(refs, blocks):
    lane = refs[0].shape[1] - PAIR
    return [(ref, row, lane) for ref in refs for row in range(0, ref.shape[0], blocks)]


def pair_keys(pairs, blocks, spot):
    lane = lax.broadcasted_iota(jnp.int32, (blocks, LANES), 1)
    block = lax.broadcasted_iota(jnp.int32, (blocks, LANES), 0)
    first = (lane < 64).astype(jnp.float32).astype(jnp.bfloat16)
    last = (lane >= 64).astype(jnp.float32).astype(jnp.bfloat16)
    hot_even = (lane == 64 + spot + block).astype(jnp.float32).astype(jnp.bfloat16)
    hot_odd = (lane == spot + block).astype(jnp.float32).astype(jnp.bfloat16)
    even, odd = [], []
    for ref, row, at in pairs:
        keys = ref[row : row + blocks, at : at + PAIR]
        middle = keys[:, LAT : LAT + LANES]
        even.append(jnp.concatenate([keys[:, :LAT], middle * first + hot_even], axis=1))
        odd.append(jnp.concatenate([middle * last + hot_odd, keys[:, LAT + LANES :]], axis=1))
    return jnp.concatenate(even, axis=0), jnp.concatenate(odd, axis=0)


def advance(query_even, query_odd, even, odd, state):
    score_even = dot(query_even, even, ((1,), (1,))) * SCORE_SCALE
    score_odd = dot(query_odd, odd, ((1,), (1,))) * SCORE_SCALE
    top = jnp.maximum(
        jnp.max(score_even, axis=-1, keepdims=True), jnp.max(score_odd, axis=-1, keepdims=True)
    )
    if state is not None:
        top = jnp.maximum(top, state[0])
    weight_even = jnp.exp(score_even - top)
    weight_odd = jnp.exp(score_odd - top)
    total = jnp.sum(weight_even, axis=-1, keepdims=True)
    total = total + jnp.sum(weight_odd, axis=-1, keepdims=True)
    sum_even = dot(weight_even.astype(jnp.bfloat16), even[:, :LAT], ((1,), (0,)))
    sum_odd = dot(weight_odd.astype(jnp.bfloat16), odd, ((1,), (0,)))
    if state is not None:
        keep = jnp.exp(state[0] - top)
        total = total + state[1] * keep
        sum_even = sum_even + state[2] * keep
        sum_odd = sum_odd + state[3] * keep
    return top, total, sum_even, sum_odd


def put_state(state, refs):
    top_ref, total_ref, even_ref, odd_ref = refs
    top_ref[...] = jnp.broadcast_to(state[0], top_ref.shape)
    total_ref[...] = jnp.broadcast_to(state[1], total_ref.shape)
    even_ref[...] = state[2]
    odd_ref[...] = state[3]


def get_state(refs):
    return (refs[0][:, :1], refs[1][:, :1], refs[2][...], refs[3][...])


def state_shapes(rows):
    f32 = jnp.float32
    return [
        jax.ShapeDtypeStruct((rows, LANES), f32),
        jax.ShapeDtypeStruct((rows, LANES), f32),
        jax.ShapeDtypeStruct((rows, LAT), f32),
        jax.ShapeDtypeStruct((rows, WIDE), f32),
    ]


def first_kernel(variants, group, *refs):
    outs = refs[-4 - 2 * variants :]
    pool_ref, other_ref = refs[:2]
    mine = [ref[0] for ref in refs[2 : -4 - 2 * variants]]
    other = [other_ref[k] for k in range(other_ref.shape[0])]
    both = jnp.concatenate([p.astype(jnp.float32) for p in mine + other], axis=0)
    bias = both[:, group * KDIM :]
    rows = both.shape[0]
    lane = lax.broadcasted_iota(jnp.int32, (rows, LANES), 1)
    for v in range(variants):
        low = bias if v == 0 else pltpu.roll(bias, LANES - 64, 1)
        high = pltpu.roll(low, 64, 1)
        for h in range(group):
            at = h // 2 * PAIR
            if h % 2 == 0:
                wide = both[:, at : at + WIDE]
                last = jnp.where(lane < 64, wide[:, LAT:], high)
                even = jnp.concatenate([wide[:, :LAT], last], axis=1)
                odd = pltpu.roll(even, 64, 1)
            else:
                wide = both[:, at + LAT : at + PAIR]
                start = jnp.where(lane < 64, low, wide[:, :LANES])
                odd = jnp.concatenate([start, wide[:, LANES:]], axis=1)
                even = pltpu.roll(odd, WIDE - 64, 1)
            outs[2 * v][h * rows : (h + 1) * rows, :] = even.astype(jnp.bfloat16)
            outs[2 * v + 1][h * rows : (h + 1) * rows, :] = odd.astype(jnp.bfloat16)
    even, odd = pair_keys(lane_pairs([pool_ref], 0), pool_ref.shape[0], 0)
    put_state(advance(outs[0][...], outs[1][...], even, odd, None), outs[2 * variants :])


def walk(queries, sources, blocks, state):
    for q, pairs in sources:
        variant, spot = divmod(q * blocks, 64)
        even, odd = pair_keys(pairs, blocks, spot)
        query_even, query_odd = queries[2 * variant : 2 * variant + 2]
        state = advance(query_even[...], query_odd[...], even, odd, state)
    return state


def middle_kernel(variants, sources, blocks, *refs):
    queries, refs = refs[: 2 * variants], refs[2 * variants :]
    state, chunks, outs = refs[:4], refs[4:-4], refs[-4:]
    sources = [(q, lane_pairs(chunks, i * blocks)) for i, q in enumerate(sources)]
    put_state(walk(queries, sources, blocks, get_state(state)), outs)


def last_kernel(variants, chips, source, blocks, *refs):
    queries, refs = refs[: 2 * variants], refs[2 * variants :]
    state, refs = refs[:4], refs[4:]
    order_ref, value_ref, proj_ref = refs[:3]
    chunks, (keep_ref, away_ref) = refs[3:-2], refs[-2:]
    own = jnp.concatenate([ref[:, : LAT + LANES] for ref in chunks[:chips]], axis=0)
    own = dot(order_ref[...], own, ((1,), (0,)))
    sources = [(source, stacked_pairs(chunks, blocks))]
    top, total, even, odd = walk(queries, sources, blocks, get_state(state))
    stats = own[:, LAT:]
    own_top = stats[:, 0:1]
    new_top = jnp.maximum(top, own_top)
    keep = jnp.exp(top - new_top)
    own_keep = jnp.exp(own_top - new_top)
    total = total * keep + (stats[:, 1:2] + stats[:, 2:3]) * own_keep
    numerator = (even + odd[:, 64 : 64 + LAT]) * keep
    numerator = numerator + own[:, :LAT] * own_keep
    context = (numerator / total).astype(jnp.bfloat16)
    heads = value_ref.shape[0]
    rows = context.shape[0] // heads
    values = [
        dot(context[h * rows : (h + 1) * rows], value_ref[h], ((1,), (0,))).astype(jnp.bfloat16)
        for h in range(heads)
    ]
    values = jnp.concatenate(values, axis=1)
    step = 1024
    half = rows // 2
    for at in range(0, proj_ref.shape[1], step):
        part = dot(values, proj_ref[:, at : at + step], ((1,), (0,)))
        keep_ref[:, at : at + step] = part[:half]
        away_ref[:, at : at + step] = part[half:].astype(jnp.bfloat16)


def expert_kernel(pos, *refs):
    blocks, (gate_ref, up_ref, down_ref, keep_ref, away_ref) = refs[:-5], refs[-5:]
    width = down_ref.shape[2]
    rows = jnp.concatenate([b[:, :width] for b in blocks], axis=0)
    gates = jnp.concatenate([b[:, width:] for b in blocks], axis=0).astype(jnp.float32)
    lane = lax.broadcasted_iota(jnp.int32, gates.shape, 1)
    gate = jnp.sum(jnp.where(lane == pos[0], gates, 0.0), axis=1, keepdims=True)
    gate_part = dot(rows, gate_ref[0], ((1,), (0,)))
    up_part = dot(rows, up_ref[0], ((1,), (0,)))
    hidden = (gate_part / (1.0 + jnp.exp(-gate_part)) * up_part).astype(jnp.bfloat16)
    half = rows.shape[0] // 2
    step = 1024
    for at in range(0, width, step):
        part = dot(hidden, down_ref[0, :, at : at + step], ((1,), (0,))) * gate
        keep_ref[:, at : at + step] = part[:half].astype(keep_ref.dtype)
        away_ref[:, at : at + step] = part[half:].astype(jnp.bfloat16)


def halve_kernel(keep_ref, away_ref, *outs):
    rows = outs[0].shape[0]
    for k, out_ref in enumerate(outs):
        at = pl.ds(k * rows, rows)
        total = keep_ref[at, :].astype(jnp.float32) + away_ref[at, :].astype(jnp.float32)
        out_ref[...] = total.astype(out_ref.dtype)


def norm_kernel(hidden_ref, gain_ref, ids_ref, weight_ref, own_ref, *refs):
    arrived, (residual_ref, row_ref) = refs[:-2], refs[-2:]
    width = hidden_ref.shape[1]
    total = own_ref[...]
    for ref in arrived:
        total = total + ref[...].astype(jnp.float32)
    total = hidden_ref[...].astype(jnp.float32) + total
    residual_ref[...] = total
    scale = lax.rsqrt(jnp.mean(total * total, axis=-1, keepdims=True) + NORM_EPS)
    row_ref[:, :width] = (total * scale * gain_ref[...].astype(jnp.float32)).astype(jnp.bfloat16)
    lane = lax.broadcasted_iota(jnp.int32, (total.shape[0], LANES), 1)
    ids, weights = ids_ref[...], weight_ref[...].astype(jnp.float32)
    gates = jnp.zeros(lane.shape, jnp.float32)
    for j in range(TOPK):
        gates = gates + jnp.where(lane == ids[:, j : j + 1], weights[:, j : j + 1], 0.0)
    row_ref[:, width:] = gates.astype(jnp.bfloat16)


def stack_kernel(*refs):
    rows = jnp.concatenate([ref[...].astype(jnp.float32) for ref in refs[:-1]], axis=0)
    refs[-1][...] = rows.astype(jnp.bfloat16)


def halve(keep, away, blocks):
    rows, width = keep.shape[0] // blocks, keep.shape[1]
    shapes = [jax.ShapeDtypeStruct((rows, width), jnp.float32)]
    shapes += [jax.ShapeDtypeStruct((rows, width), jnp.bfloat16)] * (blocks - 1)
    return vmem_call(halve_kernel, shapes, [keep, swap(away, "expert", 1)], keep.size)


def spread(rows, members, holders):
    by_z = [rows] + [swap(rows, "dp", q) for q in range(1, holders)]
    shape = jax.ShapeDtypeStruct((holders * rows.shape[0], rows.shape[1]), rows.dtype)
    by_z = vmem_call(stack_kernel, shape, by_z, rows.size)
    blocks = [by_z] + [swap(by_z, "expert", 2 * k) for k in range(1, members // 2)]
    return blocks + [swap(block, "expert", 1) for block in blocks]


def gather_sums(keep, away, members, holders):
    chips = members // 2
    rows, width = keep.shape[0] // chips, keep.shape[1]
    total, *sent = halve(keep, away, chips)
    for k in range(1, chips):
        total = total + swap(sent[k - 1], "expert", 2 * k).astype(jnp.float32)
    total = total.reshape(holders, rows // holders, width)
    sent = total.astype(jnp.bfloat16)
    result = total[0]
    for q in range(1, holders):
        result = result + swap(sent[q], "dp", q).astype(jnp.float32)
    return result


def arrival_order(chips, requests, heads):
    source = np.arange(chips * 2 * requests * heads).reshape(chips, 2, requests, heads)
    source = source.transpose(3, 1, 0, 2).reshape(-1)
    order = np.zeros((source.size, source.size), np.float32)
    order[np.arange(source.size), source] = 1.0
    return jnp.asarray(order, jnp.bfloat16)


def per_device(
    hidden_in,
    query,
    prefix_pool,
    suffix_cache,
    block_list,
    prefix_count,
    suffix_count,
    value_up,
    out_proj,
    norm_gain,
    expert_ids,
    gate_weights,
    gate_proj,
    up_proj,
    down_proj,
):
    bf16 = jnp.bfloat16
    row_count, width = hidden_in.shape
    members = lax.axis_size("expert")
    holders = lax.axis_size("dp")
    chips = members // 2
    place = lax.axis_index("expert")
    shard = lax.axis_index("dp")
    shard_blocks = prefix_pool.shape[0]
    total_blocks = shard_blocks * holders

    piece_width = prefix_pool.shape[1] // members
    piece = lax.dynamic_slice_in_dim(prefix_pool, place * piece_width, piece_width, 1)
    arrived = [None] * holders
    for q in sorted(range(1, holders), key=lambda q: (bin(q).count("1"), q)):
        low = q & -q
        arrived[q] = swap(piece if q == low else arrived[q ^ low], "dp", low)

    group_heads = HEADS // members
    variants = -(-total_blocks // 64)
    in_prefix = jnp.arange(block_list.shape[1], dtype=jnp.int32)[None, :] < prefix_count[:, None]
    slots = jnp.arange(LANES, dtype=jnp.int32)
    ids = (shard ^ (slots // shard_blocks)) * shard_blocks + slots % shard_blocks
    member = jnp.any((block_list[:, :, None] == ids) & in_prefix[:, :, None], axis=1)
    bias = jnp.where(member, 0.0, NEG_FILL).astype(bf16)
    group_width = group_heads * KDIM
    asked = []
    for k in range(chips):
        pair = [
            lax.dynamic_slice_in_dim(query, (place ^ j) * group_width, group_width, 1)
            for j in (2 * k, 2 * k + 1)
        ]
        asked.append(jnp.stack([jnp.concatenate([part, bias], axis=1) for part in pair]))
    asked = [asked[0]] + [swap(asked[k], "expert", 2 * k) for k in range(1, chips)]

    early = jnp.concatenate(arrived[1:-1])
    chunks = [early] + [swap(early, "expert", 2 * k) for k in range(1, chips)]

    pos = jnp.stack([place, shard])
    partial = jax.ShapeDtypeStruct((chips, row_count * group_heads, LAT + LANES), bf16)
    mine, other = vmem_call(
        suffix_kernel,
        [partial, partial],
        [
            pos,
            query.reshape(row_count, HEADS, KDIM),
            suffix_cache.reshape(row_count, SUFFIX, KDIM),
        ],
        4 * row_count * HEADS * SUFFIX * KDIM,
        scalars=1,
        scratch=[
            pltpu.VMEM((row_count, members, group_heads, partial.shape[2]), jnp.float32),
            pltpu.SMEM(suffix_count.shape, jnp.int32),
            pltpu.SemaphoreType.DMA,
        ],
        away=[suffix_count],
    )
    other = swap(other, "expert", 1)
    joined = jax.ShapeDtypeStruct((2 * partial.shape[1], partial.shape[2] + PAIR), bf16)
    late = list(vmem_call(join_kernel, [joined] * chips, [mine, other, arrived[-1]], mine.size))
    late[-1], chunks[1] = lax.optimization_barrier((late[-1], chunks[1]))
    late = [late[0]] + [swap(late[k], "expert", 2 * k) for k in range(1, chips)]

    rows = members * row_count * group_heads
    wide = jax.ShapeDtypeStruct((rows, WIDE), bf16)
    *queries, top, total, even, odd = vmem_call(
        functools.partial(first_kernel, variants, group_heads),
        [wide] * (2 * variants) + state_shapes(rows),
        [prefix_pool, swap(jnp.stack([part[1] for part in asked]), "expert", 1)] + asked,
        40 * rows * prefix_pool.size,
    )
    chunks += [swap(block, "expert", 1) for block in chunks]
    state = vmem_call(
        functools.partial(middle_kernel, variants, list(range(1, holders - 1)), shard_blocks),
        state_shapes(rows),
        queries + [top, total, even, odd] + chunks,
        40 * rows * prefix_pool.size,
    )
    late += [swap(block, "expert", 1) for block in late]
    half = members * row_count // 2
    keep, away = vmem_call(
        functools.partial(last_kernel, variants, chips, holders - 1, shard_blocks),
        [
            jax.ShapeDtypeStruct((half, width), jnp.float32),
            jax.ShapeDtypeStruct((half, width), bf16),
        ],
        queries
        + list(state)
        + [arrival_order(chips, row_count, group_heads), value_up, out_proj]
        + late,
        4 * rows * prefix_pool.size + 4 * half * out_proj.size,
    )
    own, *sent = halve(keep, away, chips)
    sums = [swap(sent[k - 1], "expert", 2 * k) for k in range(1, chips)]
    residual_out, token_rows = vmem_call(
        norm_kernel,
        [
            jax.ShapeDtypeStruct((row_count, width), jnp.float32),
            jax.ShapeDtypeStruct((row_count, width + LANES), bf16),
        ],
        [hidden_in, norm_gain.reshape(1, width), expert_ids, gate_weights, own] + sums,
        10 * hidden_in.size,
    )

    blocks = spread(token_rows, members, holders)
    half = blocks[0].shape[0] * chips
    keep, away = vmem_call(
        expert_kernel,
        [
            jax.ShapeDtypeStruct((half, width), jnp.float32),
            jax.ShapeDtypeStruct((half, width), bf16),
        ],
        [pos] + blocks + [gate_proj, up_proj, down_proj],
        12 * half * gate_proj.size,
        scalars=1,
    )
    moe_sum = gather_sums(keep, away, members, holders)
    return (residual_out, moe_sum)


def solution(mesh):
    in_specs = (
        P(("dp", "expert"), None),
        P(("dp", "expert"), None),
        P("dp", None),
        P(("dp", "expert"), None),
        P(("dp", "expert"), None),
        P(("dp", "expert")),
        P(("dp", "expert")),
        P("expert", None, None),
        P("expert", None),
        P(),
        P(("dp", "expert"), None),
        P(("dp", "expert"), None),
        P("expert", None, "dp"),
        P("expert", None, "dp"),
        P("expert", "dp", None),
    )
    out_specs = (P(("dp", "expert"), None), P(("dp", "expert"), None))
    return jax.shard_map(
        per_device, mesh=mesh, in_specs=in_specs, out_specs=out_specs, check_vma=False
    )
```

```python
import functools

import jax
import jax.numpy as jnp
import numpy as np
from jax import lax
from jax.experimental import pallas as pl
from jax.experimental.pallas import tpu as pltpu
from jax.sharding import PartitionSpec as P

HEADS = 64
LAT = 512
TOPK = 6
BLOCK = 64
SUFFIX = 128
KDIM = 576


NEG_FILL = -1e30
SCORE_SCALE = 192.0 ** (-0.5)
NORM_EPS = 1e-06
LANES = 128
PAIR = 2 * KDIM
WIDE = KDIM + 64


def swap(value, axis, mask):
    size = lax.axis_size(axis)
    return lax.ppermute(value, axis, [(i, i ^ mask) for i in range(size)])


def dot(a, b, dims):
    return lax.dot_general(a, b, (dims, ((), ())), preferred_element_type=jnp.float32)


def vmem_call(kernel, out_shape, operands, flops, scalars=0, scratch=(), away=(), grant=16):
    specs = [pl.BlockSpec(memory_space=pltpu.SMEM)] * scalars
    specs += [pl.BlockSpec(memory_space=pltpu.VMEM)] * (len(operands) - scalars)
    specs += [pl.BlockSpec(memory_space=pl.ANY)] * len(away)
    size = sum(o.size * o.dtype.itemsize for o in operands)
    return pl.pallas_call(
        kernel,
        out_shape=out_shape,
        in_specs=specs,
        out_specs=jax.tree.map(lambda _: pl.BlockSpec(memory_space=pltpu.VMEM), out_shape),
        scratch_shapes=list(scratch),
        cost_estimate=pl.CostEstimate(flops=flops, bytes_accessed=size, transcendentals=0),
        compiler_params=pltpu.CompilerParams(vmem_limit_bytes=grant * 1024 * 1024),
    )(*operands, *away)


def suffix_kernel(pos, query_ref, keys_ref, count_hbm, *refs):
    outs, (rows, count, sem) = refs[:-3], refs[-3:]
    copy = pltpu.make_async_copy(count_hbm, count, sem)
    copy.start()
    place = pos[0]
    requests, heads, _ = query_ref.shape
    members = 2 * len(outs)
    group = heads // members
    all_scores = [
        dot(query_ref[r], keys_ref[r], ((1,), (1,))) * SCORE_SCALE for r in range(requests)
    ]
    copy.wait()
    for r in range(requests):
        scores = all_scores[r]
        live = lax.broadcasted_iota(jnp.int32, scores.shape, 1) < count[r]
        scores = jnp.where(live, scores, NEG_FILL)
        top = jnp.max(scores, axis=-1, keepdims=True).astype(jnp.bfloat16).astype(jnp.float32)
        weights = jnp.where(live, jnp.exp(scores - top), 0.0)
        total = jnp.sum(weights, axis=-1, keepdims=True)
        high = total.astype(jnp.bfloat16).astype(jnp.float32)
        numerator = dot(weights.astype(jnp.bfloat16), keys_ref[r, :, :LAT], ((1,), (0,)))
        lane = lax.broadcasted_iota(jnp.int32, (heads, LANES), 1)
        stats = jnp.where(lane == 0, top, jnp.where(lane == 1, high, total - high))
        full = jnp.concatenate([numerator, stats], axis=1)
        for g in range(members):
            rows[r, g] = full[g * group : (g + 1) * group]
    for k, out_ref in enumerate(outs):
        taken = [rows[r, place ^ (2 * k + s)] for s in range(2) for r in range(requests)]
        out_ref[...] = jnp.concatenate(taken, axis=0).astype(jnp.bfloat16)


def join_kernel(piece_ref, *refs):
    half = len(refs) // 2
    blocks = piece_ref.shape[0]
    for rows_ref, out_ref in zip(refs[:half], refs[half:]):
        width = rows_ref.shape[1]
        out_ref[:, :width] = rows_ref[...]
        for i in range(piece_ref.shape[1] // PAIR):
            out_ref[i * blocks : (i + 1) * blocks, width:] = piece_ref[:, i * PAIR : (i + 1) * PAIR]


def lane_pairs(refs, row):
    return [(ref, row, at) for ref in refs for at in range(0, ref.shape[1], PAIR)]


def stacked_pairs(refs, blocks):
    lane = refs[0].shape[1] - PAIR
    return [(ref, row, lane) for ref in refs for row in range(0, ref.shape[0], blocks)]


def pair_keys(pairs, blocks, spot):
    lane = lax.broadcasted_iota(jnp.int32, (blocks, LANES), 1)
    block = lax.broadcasted_iota(jnp.int32, (blocks, LANES), 0)
    first = (lane < 64).astype(jnp.float32).astype(jnp.bfloat16)
    last = (lane >= 64).astype(jnp.float32).astype(jnp.bfloat16)
    hot_even = (lane == 64 + spot + block).astype(jnp.float32).astype(jnp.bfloat16)
    hot_odd = (lane == spot + block).astype(jnp.float32).astype(jnp.bfloat16)
    even, odd = [], []
    for ref, row, at in pairs:
        keys = ref[row : row + blocks, at : at + PAIR]
        middle = keys[:, LAT : LAT + LANES]
        even.append(jnp.concatenate([keys[:, :LAT], middle * first + hot_even], axis=1))
        odd.append(jnp.concatenate([middle * last + hot_odd, keys[:, LAT + LANES :]], axis=1))
    return jnp.concatenate(even, axis=0), jnp.concatenate(odd, axis=0)


def advance(query_even, query_odd, even, odd, state):
    score_even = dot(query_even, even, ((1,), (1,))) * SCORE_SCALE
    score_odd = dot(query_odd, odd, ((1,), (1,))) * SCORE_SCALE
    top = jnp.maximum(
        jnp.max(score_even, axis=-1, keepdims=True), jnp.max(score_odd, axis=-1, keepdims=True)
    )
    if state is not None:
        top = jnp.maximum(top, state[0])
    weight_even = jnp.exp(score_even - top)
    weight_odd = jnp.exp(score_odd - top)
    total = jnp.sum(weight_even, axis=-1, keepdims=True)
    total = total + jnp.sum(weight_odd, axis=-1, keepdims=True)
    sum_even = dot(weight_even.astype(jnp.bfloat16), even[:, :LAT], ((1,), (0,)))
    sum_odd = dot(weight_odd.astype(jnp.bfloat16), odd, ((1,), (0,)))
    if state is not None:
        keep = jnp.exp(state[0] - top)
        total = total + state[1] * keep
        sum_even = sum_even + state[2] * keep
        sum_odd = sum_odd + state[3] * keep
    return top, total, sum_even, sum_odd


def put_state(state, refs):
    top_ref, total_ref, even_ref, odd_ref = refs
    top_ref[...] = jnp.broadcast_to(state[0], top_ref.shape)
    total_ref[...] = jnp.broadcast_to(state[1], total_ref.shape)
    even_ref[...] = state[2]
    odd_ref[...] = state[3]


def get_state(refs):
    return (refs[0][:, :1], refs[1][:, :1], refs[2][...], refs[3][...])


def state_shapes(rows):
    f32 = jnp.float32
    return [
        jax.ShapeDtypeStruct((rows, LANES), f32),
        jax.ShapeDtypeStruct((rows, LANES), f32),
        jax.ShapeDtypeStruct((rows, LAT), f32),
        jax.ShapeDtypeStruct((rows, WIDE), f32),
    ]


def first_kernel(variants, group, *refs):
    outs = refs[-4 - 2 * variants :]
    pool_ref, other_ref = refs[:2]
    mine = [ref[0] for ref in refs[2 : -4 - 2 * variants]]
    other = [other_ref[k] for k in range(other_ref.shape[0])]
    both = jnp.concatenate([p.astype(jnp.float32) for p in mine + other], axis=0)
    bias = both[:, group * KDIM :]
    rows = both.shape[0]
    lane = lax.broadcasted_iota(jnp.int32, (rows, LANES), 1)
    for v in range(variants):
        low = bias if v == 0 else pltpu.roll(bias, LANES - 64, 1)
        high = pltpu.roll(low, 64, 1)
        for h in range(group):
            at = h // 2 * PAIR
            if h % 2 == 0:
                wide = both[:, at : at + WIDE]
                last = jnp.where(lane < 64, wide[:, LAT:], high)
                even = jnp.concatenate([wide[:, :LAT], last], axis=1)
                odd = pltpu.roll(even, 64, 1)
            else:
                wide = both[:, at + LAT : at + PAIR]
                start = jnp.where(lane < 64, low, wide[:, :LANES])
                odd = jnp.concatenate([start, wide[:, LANES:]], axis=1)
                even = pltpu.roll(odd, WIDE - 64, 1)
            outs[2 * v][h * rows : (h + 1) * rows, :] = even.astype(jnp.bfloat16)
            outs[2 * v + 1][h * rows : (h + 1) * rows, :] = odd.astype(jnp.bfloat16)
    even, odd = pair_keys(lane_pairs([pool_ref], 0), pool_ref.shape[0], 0)
    put_state(advance(outs[0][...], outs[1][...], even, odd, None), outs[2 * variants :])


def walk(queries, sources, blocks, state):
    for q, pairs in sources:
        variant, spot = divmod(q * blocks, 64)
        even, odd = pair_keys(pairs, blocks, spot)
        query_even, query_odd = queries[2 * variant : 2 * variant + 2]
        state = advance(query_even[...], query_odd[...], even, odd, state)
    return state


def middle_kernel(variants, sources, blocks, *refs):
    queries, refs = refs[: 2 * variants], refs[2 * variants :]
    state, chunks, outs = refs[:4], refs[4:-4], refs[-4:]
    each = chunks[0].shape[0]
    places = [(ref, row) for ref in chunks for row in range(0, ref.shape[0], each)]
    sources = [
        (q, [pair for ref, row in places for pair in lane_pairs([ref], row + i * blocks)])
        for i, q in enumerate(sources)
    ]
    put_state(walk(queries, sources, blocks, get_state(state)), outs)


def last_kernel(variants, chips, source, blocks, *refs):
    queries, refs = refs[: 2 * variants], refs[2 * variants :]
    state, refs = refs[:4], refs[4:]
    order_ref, value_ref, proj_ref = refs[:3]
    chunks, (keep_ref, away_ref) = refs[3:-2], refs[-2:]
    half = chunks[0].shape[0] // 2
    own = []
    for k in range(chips):
        own.append(chunks[k][:half, : LAT + LANES].astype(jnp.float32))
        own.append(chunks[chips + k][half:, : LAT + LANES].astype(jnp.float32))
    own = dot(order_ref[...], jnp.concatenate(own, axis=0).astype(jnp.bfloat16), ((1,), (0,)))
    sources = [(source, stacked_pairs(chunks, blocks))]
    top, total, even, odd = walk(queries, sources, blocks, get_state(state))
    stats = own[:, LAT:]
    own_top = stats[:, 0:1]
    new_top = jnp.maximum(top, own_top)
    keep = jnp.exp(top - new_top)
    own_keep = jnp.exp(own_top - new_top)
    total = total * keep + (stats[:, 1:2] + stats[:, 2:3]) * own_keep
    numerator = (even + odd[:, 64 : 64 + LAT]) * keep
    numerator = numerator + own[:, :LAT] * own_keep
    context = (numerator / total).astype(jnp.bfloat16)
    heads = value_ref.shape[0]
    rows = context.shape[0] // heads
    values = [
        dot(context[h * rows : (h + 1) * rows], value_ref[h], ((1,), (0,))).astype(jnp.bfloat16)
        for h in range(heads)
    ]
    values = jnp.concatenate(values, axis=1)
    step = 1024
    half = rows // 2
    for at in range(0, proj_ref.shape[1], step):
        part = dot(values, proj_ref[:, at : at + step], ((1,), (0,)))
        keep_ref[:, at : at + step] = part[:half]
        away_ref[:, at : at + step] = part[half:].astype(jnp.bfloat16)


def expert_kernel(pos, *refs):
    blocks, (gate_ref, up_ref, down_ref, keep_ref, away_ref) = refs[:-5], refs[-5:]
    width = down_ref.shape[2]
    rows = jnp.concatenate([b[:, :width] for b in blocks], axis=0)
    gates = jnp.concatenate([b[:, width:] for b in blocks], axis=0).astype(jnp.float32)
    lane = lax.broadcasted_iota(jnp.int32, gates.shape, 1)
    gate = jnp.sum(jnp.where(lane == pos[0], gates, 0.0), axis=1, keepdims=True)
    gate_part = dot(rows, gate_ref[0], ((1,), (0,)))
    up_part = dot(rows, up_ref[0], ((1,), (0,)))
    hidden = (gate_part / (1.0 + jnp.exp(-gate_part)) * up_part).astype(jnp.bfloat16)
    half = rows.shape[0] // 2
    step = 1024
    for at in range(0, width, step):
        part = dot(hidden, down_ref[0, :, at : at + step], ((1,), (0,))) * gate
        keep_ref[:, at : at + step] = part[:half].astype(keep_ref.dtype)
        away_ref[:, at : at + step] = part[half:].astype(jnp.bfloat16)


def halve_kernel(keep_ref, away_ref, *outs):
    rows = outs[0].shape[0]
    for k, out_ref in enumerate(outs):
        at = pl.ds(k * rows, rows)
        total = keep_ref[at, :].astype(jnp.float32) + away_ref[at, :].astype(jnp.float32)
        out_ref[...] = total.astype(out_ref.dtype)


def norm_kernel(hidden_ref, gain_ref, ids_ref, weight_ref, own_ref, *refs):
    arrived, (residual_ref, row_ref) = refs[:-2], refs[-2:]
    width = hidden_ref.shape[1]
    total = own_ref[...]
    for ref in arrived:
        total = total + ref[...].astype(jnp.float32)
    total = hidden_ref[...].astype(jnp.float32) + total
    residual_ref[...] = total
    scale = lax.rsqrt(jnp.mean(total * total, axis=-1, keepdims=True) + NORM_EPS)
    row_ref[:, :width] = (total * scale * gain_ref[...].astype(jnp.float32)).astype(jnp.bfloat16)
    lane = lax.broadcasted_iota(jnp.int32, (total.shape[0], LANES), 1)
    ids, weights = ids_ref[...], weight_ref[...].astype(jnp.float32)
    gates = jnp.zeros(lane.shape, jnp.float32)
    for j in range(TOPK):
        gates = gates + jnp.where(lane == ids[:, j : j + 1], weights[:, j : j + 1], 0.0)
    row_ref[:, width:] = gates.astype(jnp.bfloat16)


def pile_kernel(*refs):
    rows = refs[0].shape[0]
    for i, ref in enumerate(refs[:-1]):
        refs[-1][i * rows : (i + 1) * rows, :] = ref[...]


def stack_kernel(*refs):
    rows = jnp.concatenate([ref[...].astype(jnp.float32) for ref in refs[:-1]], axis=0)
    refs[-1][...] = rows.astype(jnp.bfloat16)


def halve(keep, away, blocks):
    rows, width = keep.shape[0] // blocks, keep.shape[1]
    shapes = [jax.ShapeDtypeStruct((rows, width), jnp.float32)]
    shapes += [jax.ShapeDtypeStruct((rows, width), jnp.bfloat16)] * (blocks - 1)
    return vmem_call(halve_kernel, shapes, [keep, swap(away, "expert", 1)], keep.size)


def spread(rows, members, holders):
    by_z = [rows] + [swap(rows, "dp", q) for q in range(1, holders)]
    shape = jax.ShapeDtypeStruct((holders * rows.shape[0], rows.shape[1]), rows.dtype)
    by_z = vmem_call(stack_kernel, shape, by_z, rows.size)
    blocks = [by_z] + [swap(by_z, "expert", 2 * k) for k in range(1, members // 2)]
    return blocks + [swap(block, "expert", 1) for block in blocks]


def gather_sums(keep, away, members, holders):
    chips = members // 2
    rows, width = keep.shape[0] // chips, keep.shape[1]
    total, *sent = halve(keep, away, chips)
    for k in range(1, chips):
        total = total + swap(sent[k - 1], "expert", 2 * k).astype(jnp.float32)
    total = total.reshape(holders, rows // holders, width)
    sent = total.astype(jnp.bfloat16)
    result = total[0]
    for q in range(1, holders):
        result = result + swap(sent[q], "dp", q).astype(jnp.float32)
    return result


def arrival_order(chips, requests, heads):
    source = np.arange(chips * 2 * requests * heads).reshape(chips, 2, requests, heads)
    source = source.transpose(3, 1, 0, 2).reshape(-1)
    order = np.zeros((source.size, source.size), np.float32)
    order[np.arange(source.size), source] = 1.0
    return jnp.asarray(order, jnp.bfloat16)


def per_device(
    hidden_in,
    query,
    prefix_pool,
    suffix_cache,
    block_list,
    prefix_count,
    suffix_count,
    value_up,
    out_proj,
    norm_gain,
    expert_ids,
    gate_weights,
    gate_proj,
    up_proj,
    down_proj,
):
    bf16 = jnp.bfloat16
    row_count, width = hidden_in.shape
    members = lax.axis_size("expert")
    holders = lax.axis_size("dp")
    chips = members // 2
    place = lax.axis_index("expert")
    shard = lax.axis_index("dp")
    shard_blocks = prefix_pool.shape[0]
    total_blocks = shard_blocks * holders

    piece_width = prefix_pool.shape[1] // members
    piece = lax.dynamic_slice_in_dim(prefix_pool, place * piece_width, piece_width, 1)
    arrived = [None] * holders
    for q in sorted(range(1, holders), key=lambda q: (bin(q).count("1"), q)):
        low = q & -q
        arrived[q] = swap(piece if q == low else arrived[q ^ low], "dp", low)

    group_heads = HEADS // members
    variants = -(-total_blocks // 64)
    in_prefix = jnp.arange(block_list.shape[1], dtype=jnp.int32)[None, :] < prefix_count[:, None]
    slots = jnp.arange(LANES, dtype=jnp.int32)
    ids = (shard ^ (slots // shard_blocks)) * shard_blocks + slots % shard_blocks
    member = jnp.any((block_list[:, :, None] == ids) & in_prefix[:, :, None], axis=1)
    bias = jnp.where(member, 0.0, NEG_FILL).astype(bf16)
    group_width = group_heads * KDIM
    asked = []
    for k in range(chips):
        pair = [
            lax.dynamic_slice_in_dim(query, (place ^ j) * group_width, group_width, 1)
            for j in (2 * k, 2 * k + 1)
        ]
        asked.append(jnp.stack([jnp.concatenate([part, bias], axis=1) for part in pair]))
    asked = [asked[0]] + [swap(asked[k], "expert", 2 * k) for k in range(1, chips)]

    early = jnp.concatenate(arrived[1:-1])
    chunks = [early] + [swap(early, "expert", 2 * k) for k in range(1, chips - 1)]
    *asked, early = lax.optimization_barrier((*asked, early))
    chunks.append(swap(early, "expert", 2 * (chips - 1)))

    pos = jnp.stack([place, shard])
    query, suffix_cache, early = lax.optimization_barrier((query, suffix_cache, early))
    partial = jax.ShapeDtypeStruct((2 * row_count * group_heads, LAT + LANES), bf16)
    partials = vmem_call(
        suffix_kernel,
        [partial] * chips,
        [
            pos,
            query.reshape(row_count, HEADS, KDIM),
            suffix_cache.reshape(row_count, SUFFIX, KDIM),
        ],
        4 * row_count * HEADS * SUFFIX * KDIM,
        scalars=1,
        scratch=[
            pltpu.VMEM((row_count, members, group_heads, partial.shape[1]), jnp.float32),
            pltpu.SMEM(suffix_count.shape, jnp.int32),
            pltpu.SemaphoreType.DMA,
        ],
        away=[suffix_count],
    )
    joined = jax.ShapeDtypeStruct((partial.shape[0], partial.shape[1] + PAIR), bf16)
    late = list(
        vmem_call(join_kernel, [joined] * chips, [arrived[-1]] + list(partials), piece.size)
    )
    late = [late[0]] + [swap(late[k], "expert", 2 * k) for k in range(1, chips)]

    rows = members * row_count * group_heads
    wide = jax.ShapeDtypeStruct((rows, WIDE), bf16)
    *queries, top, total, even, odd = vmem_call(
        functools.partial(first_kernel, variants, group_heads),
        [wide] * (2 * variants) + state_shapes(rows),
        [prefix_pool, swap(jnp.stack([part[1] for part in asked]), "expert", 1)]
        + asked,
        40 * rows * prefix_pool.size,
    )
    *chunks, late[1], late[2] = lax.optimization_barrier((*chunks, late[1], late[2]))
    held = vmem_call(
        pile_kernel,
        jax.ShapeDtypeStruct((chips * early.shape[0], early.shape[1]), bf16),
        chunks,
        chips * early.size,
    )
    chunks.append(swap(held, "expert", 1))
    state = vmem_call(
        functools.partial(middle_kernel, variants, list(range(1, holders - 1)), shard_blocks),
        state_shapes(rows),
        queries + [top, total, even, odd] + chunks,
        40 * rows * prefix_pool.size,
    )
    *held, top = lax.optimization_barrier((*late, state[0]))
    state = [top, *state[1:]]
    late = held + [swap(block, "expert", 1) for block in held]
    half = members * row_count // 2
    keep, away = vmem_call(
        functools.partial(last_kernel, variants, chips, holders - 1, shard_blocks),
        [
            jax.ShapeDtypeStruct((half, width), jnp.float32),
            jax.ShapeDtypeStruct((half, width), bf16),
        ],
        queries
        + list(state)
        + [arrival_order(chips, row_count, group_heads), value_up, out_proj]
        + late,
        4 * rows * prefix_pool.size + 4 * half * out_proj.size,
    )
    own, *sent = halve(keep, away, chips)
    sums = [swap(sent[k - 1], "expert", 2 * k) for k in range(1, chips)]
    residual_out, token_rows = vmem_call(
        norm_kernel,
        [
            jax.ShapeDtypeStruct((row_count, width), jnp.float32),
            jax.ShapeDtypeStruct((row_count, width + LANES), bf16),
        ],
        [hidden_in, norm_gain.reshape(1, width), expert_ids, gate_weights, own] + sums,
        10 * hidden_in.size,
    )

    blocks = spread(token_rows, members, holders)
    half = blocks[0].shape[0] * chips
    keep, away = vmem_call(
        expert_kernel,
        [
            jax.ShapeDtypeStruct((half, width), jnp.float32),
            jax.ShapeDtypeStruct((half, width), bf16),
        ],
        [pos] + blocks + [gate_proj, up_proj, down_proj],
        12 * half * gate_proj.size,
        scalars=1,
    )
    moe_sum = gather_sums(keep, away, members, holders)
    return (residual_out, moe_sum)


def solution(mesh):
    in_specs = (
        P(("dp", "expert"), None),
        P(("dp", "expert"), None),
        P("dp", None),
        P(("dp", "expert"), None),
        P(("dp", "expert"), None),
        P(("dp", "expert")),
        P(("dp", "expert")),
        P("expert", None, None),
        P("expert", None),
        P(),
        P(("dp", "expert"), None),
        P(("dp", "expert"), None),
        P("expert", None, "dp"),
        P("expert", None, "dp"),
        P("expert", "dp", None),
    )
    out_specs = (P(("dp", "expert"), None), P(("dp", "expert"), None))
    return jax.shard_map(
        per_device, mesh=mesh, in_specs=in_specs, out_specs=out_specs, check_vma=False
    )
```

```python
import functools

import jax
import jax.numpy as jnp
import numpy as np
from jax import lax
from jax.experimental import pallas as pl
from jax.experimental.pallas import tpu as pltpu
from jax.sharding import PartitionSpec as P

HEADS = 64
LAT = 512
TOPK = 6
BLOCK = 64
SUFFIX = 128
KDIM = 576


NEG_FILL = -1e30
SCORE_SCALE = 192.0 ** (-0.5)
NORM_EPS = 1e-06
LANES = 128
PAIR = 2 * KDIM
WIDE = KDIM + 64


def swap(value, axis, mask):
    size = lax.axis_size(axis)
    return lax.ppermute(value, axis, [(i, i ^ mask) for i in range(size)])


def dot(a, b, dims):
    return lax.dot_general(a, b, (dims, ((), ())), preferred_element_type=jnp.float32)


def vmem_call(kernel, out_shape, operands, flops, scalars=0, scratch=(), away=(), grant=16):
    specs = [pl.BlockSpec(memory_space=pltpu.SMEM)] * scalars
    specs += [pl.BlockSpec(memory_space=pltpu.VMEM)] * (len(operands) - scalars)
    specs += [pl.BlockSpec(memory_space=pl.ANY)] * len(away)
    size = sum(o.size * o.dtype.itemsize for o in operands)
    return pl.pallas_call(
        kernel,
        out_shape=out_shape,
        in_specs=specs,
        out_specs=jax.tree.map(lambda _: pl.BlockSpec(memory_space=pltpu.VMEM), out_shape),
        scratch_shapes=list(scratch),
        cost_estimate=pl.CostEstimate(flops=flops, bytes_accessed=size, transcendentals=0),
        compiler_params=pltpu.CompilerParams(vmem_limit_bytes=grant * 1024 * 1024),
    )(*operands, *away)


def suffix_kernel(pos, query_ref, keys_ref, count_hbm, *refs):
    outs, (rows, count, sem) = refs[:-3], refs[-3:]
    copy = pltpu.make_async_copy(count_hbm, count, sem)
    copy.start()
    place = pos[0]
    requests, heads, _ = query_ref.shape
    members = 2 * len(outs)
    group = heads // members
    all_scores = [
        dot(query_ref[r], keys_ref[r], ((1,), (1,))) * SCORE_SCALE for r in range(requests)
    ]
    copy.wait()
    for r in range(requests):
        scores = all_scores[r]
        live = lax.broadcasted_iota(jnp.int32, scores.shape, 1) < count[r]
        scores = jnp.where(live, scores, NEG_FILL)
        top = jnp.max(scores, axis=-1, keepdims=True).astype(jnp.bfloat16).astype(jnp.float32)
        weights = jnp.where(live, jnp.exp(scores - top), 0.0)
        total = jnp.sum(weights, axis=-1, keepdims=True)
        high = total.astype(jnp.bfloat16).astype(jnp.float32)
        numerator = dot(weights.astype(jnp.bfloat16), keys_ref[r, :, :LAT], ((1,), (0,)))
        lane = lax.broadcasted_iota(jnp.int32, (heads, LANES), 1)
        stats = jnp.where(lane == 0, top, jnp.where(lane == 1, high, total - high))
        full = jnp.concatenate([numerator, stats], axis=1)
        for g in range(members):
            rows[r, g] = full[g * group : (g + 1) * group]
    for k, out_ref in enumerate(outs):
        taken = [rows[r, place ^ (2 * k + s)] for s in range(2) for r in range(requests)]
        out_ref[...] = jnp.concatenate(taken, axis=0).astype(jnp.bfloat16)


def join_kernel(piece_ref, *refs):
    half = len(refs) // 2
    blocks = piece_ref.shape[0]
    for rows_ref, out_ref in zip(refs[:half], refs[half:]):
        width = rows_ref.shape[1]
        out_ref[:, :width] = rows_ref[...]
        for i in range(piece_ref.shape[1] // PAIR):
            out_ref[i * blocks : (i + 1) * blocks, width:] = piece_ref[:, i * PAIR : (i + 1) * PAIR]


def lane_pairs(refs, row):
    return [(ref, row, at) for ref in refs for at in range(0, ref.shape[1], PAIR)]


def stacked_pairs(refs, blocks):
    lane = refs[0].shape[1] - PAIR
    return [(ref, row, lane) for ref in refs for row in range(0, ref.shape[0], blocks)]


def pair_keys(pairs, blocks, spot):
    lane = lax.broadcasted_iota(jnp.int32, (blocks, LANES), 1)
    block = lax.broadcasted_iota(jnp.int32, (blocks, LANES), 0)
    first = (lane < 64).astype(jnp.float32).astype(jnp.bfloat16)
    last = (lane >= 64).astype(jnp.float32).astype(jnp.bfloat16)
    hot_even = (lane == 64 + spot + block).astype(jnp.float32).astype(jnp.bfloat16)
    hot_odd = (lane == spot + block).astype(jnp.float32).astype(jnp.bfloat16)
    even, odd = [], []
    for ref, row, at in pairs:
        keys = ref[row : row + blocks, at : at + PAIR]
        middle = keys[:, LAT : LAT + LANES]
        even.append(jnp.concatenate([keys[:, :LAT], middle * first + hot_even], axis=1))
        odd.append(jnp.concatenate([middle * last + hot_odd, keys[:, LAT + LANES :]], axis=1))
    return jnp.concatenate(even, axis=0), jnp.concatenate(odd, axis=0)


def advance(query_even, query_odd, even, odd, state):
    score_even = dot(query_even, even, ((1,), (1,))) * SCORE_SCALE
    score_odd = dot(query_odd, odd, ((1,), (1,))) * SCORE_SCALE
    top = jnp.maximum(
        jnp.max(score_even, axis=-1, keepdims=True), jnp.max(score_odd, axis=-1, keepdims=True)
    )
    if state is not None:
        top = jnp.maximum(top, state[0])
    weight_even = jnp.exp(score_even - top)
    weight_odd = jnp.exp(score_odd - top)
    total = jnp.sum(weight_even, axis=-1, keepdims=True)
    total = total + jnp.sum(weight_odd, axis=-1, keepdims=True)
    sum_even = dot(weight_even.astype(jnp.bfloat16), even[:, :LAT], ((1,), (0,)))
    sum_odd = dot(weight_odd.astype(jnp.bfloat16), odd, ((1,), (0,)))
    if state is not None:
        keep = jnp.exp(state[0] - top)
        total = total + state[1] * keep
        sum_even = sum_even + state[2] * keep
        sum_odd = sum_odd + state[3] * keep
    return top, total, sum_even, sum_odd


def put_state(state, refs):
    top_ref, total_ref, even_ref, odd_ref = refs
    top_ref[...] = jnp.broadcast_to(state[0], top_ref.shape)
    total_ref[...] = jnp.broadcast_to(state[1], total_ref.shape)
    even_ref[...] = state[2]
    odd_ref[...] = state[3]


def get_state(refs):
    return (refs[0][:, :1], refs[1][:, :1], refs[2][...], refs[3][...])


def state_shapes(rows):
    f32 = jnp.float32
    return [
        jax.ShapeDtypeStruct((rows, LANES), f32),
        jax.ShapeDtypeStruct((rows, LANES), f32),
        jax.ShapeDtypeStruct((rows, LAT), f32),
        jax.ShapeDtypeStruct((rows, WIDE), f32),
    ]


def first_kernel(variants, group, *refs):
    outs = refs[-4 - 2 * variants :]
    pool_ref, other_ref = refs[:2]
    mine = [ref[0] for ref in refs[2 : -4 - 2 * variants]]
    other = [other_ref[k] for k in range(other_ref.shape[0])]
    both = jnp.concatenate([p.astype(jnp.float32) for p in mine + other], axis=0)
    bias = both[:, group * KDIM :]
    rows = both.shape[0]
    lane = lax.broadcasted_iota(jnp.int32, (rows, LANES), 1)
    for v in range(variants):
        low = bias if v == 0 else pltpu.roll(bias, LANES - 64, 1)
        high = pltpu.roll(low, 64, 1)
        for h in range(group):
            at = h // 2 * PAIR
            if h % 2 == 0:
                wide = both[:, at : at + WIDE]
                last = jnp.where(lane < 64, wide[:, LAT:], high)
                even = jnp.concatenate([wide[:, :LAT], last], axis=1)
                odd = pltpu.roll(even, 64, 1)
            else:
                wide = both[:, at + LAT : at + PAIR]
                start = jnp.where(lane < 64, low, wide[:, :LANES])
                odd = jnp.concatenate([start, wide[:, LANES:]], axis=1)
                even = pltpu.roll(odd, WIDE - 64, 1)
            outs[2 * v][h * rows : (h + 1) * rows, :] = even.astype(jnp.bfloat16)
            outs[2 * v + 1][h * rows : (h + 1) * rows, :] = odd.astype(jnp.bfloat16)
    even, odd = pair_keys(lane_pairs([pool_ref], 0), pool_ref.shape[0], 0)
    put_state(advance(outs[0][...], outs[1][...], even, odd, None), outs[2 * variants :])


def walk(queries, sources, blocks, state):
    for q, pairs in sources:
        variant, spot = divmod(q * blocks, 64)
        even, odd = pair_keys(pairs, blocks, spot)
        query_even, query_odd = queries[2 * variant : 2 * variant + 2]
        state = advance(query_even[...], query_odd[...], even, odd, state)
    return state


def middle_kernel(variants, sources, blocks, *refs):
    queries, refs = refs[: 2 * variants], refs[2 * variants :]
    state, chunks, outs = refs[:4], refs[4:-4], refs[-4:]
    each = chunks[0].shape[0]
    places = [(ref, row) for ref in chunks for row in range(0, ref.shape[0], each)]
    sources = [
        (q, [pair for ref, row in places for pair in lane_pairs([ref], row + i * blocks)])
        for i, q in enumerate(sources)
    ]
    put_state(walk(queries, sources, blocks, get_state(state)), outs)


def last_kernel(variants, chips, source, blocks, *refs):
    queries, refs = refs[: 2 * variants], refs[2 * variants :]
    state, refs = refs[:4], refs[4:]
    order_ref, value_ref, proj_ref = refs[:3]
    chunks, (keep_ref, away_ref) = refs[3:-2], refs[-2:]
    half = chunks[0].shape[0] // 2
    own = []
    for k in range(chips):
        own.append(chunks[k][:half, : LAT + LANES].astype(jnp.float32))
        own.append(chunks[chips + k][half:, : LAT + LANES].astype(jnp.float32))
    own = dot(order_ref[...], jnp.concatenate(own, axis=0).astype(jnp.bfloat16), ((1,), (0,)))
    sources = [(source, stacked_pairs(chunks, blocks))]
    top, total, even, odd = walk(queries, sources, blocks, get_state(state))
    stats = own[:, LAT:]
    own_top = stats[:, 0:1]
    new_top = jnp.maximum(top, own_top)
    keep = jnp.exp(top - new_top)
    own_keep = jnp.exp(own_top - new_top)
    total = total * keep + (stats[:, 1:2] + stats[:, 2:3]) * own_keep
    numerator = (even + odd[:, 64 : 64 + LAT]) * keep
    numerator = numerator + own[:, :LAT] * own_keep
    context = (numerator / total).astype(jnp.bfloat16)
    heads = value_ref.shape[0]
    rows = context.shape[0] // heads
    values = [
        dot(context[h * rows : (h + 1) * rows], value_ref[h], ((1,), (0,))).astype(jnp.bfloat16)
        for h in range(heads)
    ]
    values = jnp.concatenate(values, axis=1)
    step = 1024
    half = rows // 2
    for at in range(0, proj_ref.shape[1], step):
        part = dot(values, proj_ref[:, at : at + step], ((1,), (0,)))
        keep_ref[:, at : at + step] = part[:half]
        away_ref[:, at : at + step] = part[half:].astype(jnp.bfloat16)


def expert_kernel(pos, *refs):
    blocks, (gate_ref, up_ref, down_ref, keep_ref, away_ref) = refs[:-5], refs[-5:]
    width = down_ref.shape[2]
    rows = jnp.concatenate([b[:, :width] for b in blocks], axis=0)
    gates = jnp.concatenate([b[:, width:] for b in blocks], axis=0).astype(jnp.float32)
    lane = lax.broadcasted_iota(jnp.int32, gates.shape, 1)
    gate = jnp.sum(jnp.where(lane == pos[0], gates, 0.0), axis=1, keepdims=True)
    gate_part = dot(rows, gate_ref[0], ((1,), (0,)))
    up_part = dot(rows, up_ref[0], ((1,), (0,)))
    hidden = (gate_part / (1.0 + jnp.exp(-gate_part)) * up_part).astype(jnp.bfloat16)
    half = rows.shape[0] // 2
    step = 1024
    for at in range(0, width, step):
        part = dot(hidden, down_ref[0, :, at : at + step], ((1,), (0,))) * gate
        keep_ref[:, at : at + step] = part[:half].astype(keep_ref.dtype)
        away_ref[:, at : at + step] = part[half:].astype(jnp.bfloat16)


def halve_kernel(keep_ref, away_ref, *outs):
    rows = outs[0].shape[0]
    for k, out_ref in enumerate(outs):
        at = pl.ds(k * rows, rows)
        total = keep_ref[at, :].astype(jnp.float32) + away_ref[at, :].astype(jnp.float32)
        out_ref[...] = total.astype(out_ref.dtype)


def norm_kernel(hidden_ref, gain_ref, ids_ref, weight_ref, own_ref, *refs):
    arrived, (residual_ref, row_ref) = refs[:-2], refs[-2:]
    width = hidden_ref.shape[1]
    total = own_ref[...]
    for ref in arrived:
        total = total + ref[...].astype(jnp.float32)
    total = hidden_ref[...].astype(jnp.float32) + total
    residual_ref[...] = total
    scale = lax.rsqrt(jnp.mean(total * total, axis=-1, keepdims=True) + NORM_EPS)
    row_ref[:, :width] = (total * scale * gain_ref[...].astype(jnp.float32)).astype(jnp.bfloat16)
    lane = lax.broadcasted_iota(jnp.int32, (total.shape[0], LANES), 1)
    ids, weights = ids_ref[...], weight_ref[...].astype(jnp.float32)
    gates = jnp.zeros(lane.shape, jnp.float32)
    for j in range(TOPK):
        gates = gates + jnp.where(lane == ids[:, j : j + 1], weights[:, j : j + 1], 0.0)
    row_ref[:, width:] = gates.astype(jnp.bfloat16)


def pile_kernel(*refs):
    rows = refs[0].shape[0]
    for i, ref in enumerate(refs[:-1]):
        refs[-1][i * rows : (i + 1) * rows, :] = ref[...]


def stack_kernel(*refs):
    rows = jnp.concatenate([ref[...].astype(jnp.float32) for ref in refs[:-1]], axis=0)
    refs[-1][...] = rows.astype(jnp.bfloat16)


def halve(keep, away, blocks):
    rows, width = keep.shape[0] // blocks, keep.shape[1]
    shapes = [jax.ShapeDtypeStruct((rows, width), jnp.float32)]
    shapes += [jax.ShapeDtypeStruct((rows, width), jnp.bfloat16)] * (blocks - 1)
    return vmem_call(halve_kernel, shapes, [keep, swap(away, "expert", 1)], keep.size)


def spread(rows, members, holders):
    by_z = [swap(rows, "dp", q) for q in reversed(range(1, holders))]
    by_z = [rows] + by_z[::-1]
    shape = jax.ShapeDtypeStruct((holders * rows.shape[0], rows.shape[1]), rows.dtype)
    by_z = vmem_call(stack_kernel, shape, by_z, rows.size)
    blocks = [swap(by_z, "expert", 2 * k) for k in reversed(range(1, members // 2))]
    blocks = [by_z] + blocks[::-1]
    return blocks + [swap(block, "expert", 1) for block in blocks]


def gather_sums(keep, away, members, holders):
    chips = members // 2
    rows, width = keep.shape[0] // chips, keep.shape[1]
    total, *sent = halve(keep, away, chips)
    for k in reversed(range(1, chips)):
        total = total + swap(sent[k - 1], "expert", 2 * k).astype(jnp.float32)
    total = total.reshape(holders, rows // holders, width)
    sent = total.astype(jnp.bfloat16)
    result = total[0]
    for q in reversed(range(1, holders)):
        result = result + swap(sent[q], "dp", q).astype(jnp.float32)
    return result


def arrival_order(chips, requests, heads):
    source = np.arange(chips * 2 * requests * heads).reshape(chips, 2, requests, heads)
    source = source.transpose(3, 1, 0, 2).reshape(-1)
    order = np.zeros((source.size, source.size), np.float32)
    order[np.arange(source.size), source] = 1.0
    return jnp.asarray(order, jnp.bfloat16)


def per_device(
    hidden_in,
    query,
    prefix_pool,
    suffix_cache,
    block_list,
    prefix_count,
    suffix_count,
    value_up,
    out_proj,
    norm_gain,
    expert_ids,
    gate_weights,
    gate_proj,
    up_proj,
    down_proj,
):
    bf16 = jnp.bfloat16
    row_count, width = hidden_in.shape
    members = lax.axis_size("expert")
    holders = lax.axis_size("dp")
    chips = members // 2
    place = lax.axis_index("expert")
    shard = lax.axis_index("dp")
    shard_blocks = prefix_pool.shape[0]
    total_blocks = shard_blocks * holders

    piece_width = prefix_pool.shape[1] // members
    piece = lax.dynamic_slice_in_dim(prefix_pool, place * piece_width, piece_width, 1)
    arrived = [None] * holders
    for q in sorted(range(1, holders), key=lambda q: (bin(q).count("1"), q)):
        low = q & -q
        arrived[q] = swap(piece if q == low else arrived[q ^ low], "dp", low)

    group_heads = HEADS // members
    variants = -(-total_blocks // 64)
    in_prefix = jnp.arange(block_list.shape[1], dtype=jnp.int32)[None, :] < prefix_count[:, None]
    slots = jnp.arange(LANES, dtype=jnp.int32)
    ids = (shard ^ (slots // shard_blocks)) * shard_blocks + slots % shard_blocks
    member = jnp.any((block_list[:, :, None] == ids) & in_prefix[:, :, None], axis=1)
    bias = jnp.where(member, 0.0, NEG_FILL).astype(bf16)
    group_width = group_heads * KDIM
    asked = []
    for k in range(chips):
        pair = [
            lax.dynamic_slice_in_dim(query, (place ^ j) * group_width, group_width, 1)
            for j in (2 * k, 2 * k + 1)
        ]
        asked.append(jnp.stack([jnp.concatenate([part, bias], axis=1) for part in pair]))
    asked = [asked[0]] + [swap(asked[k], "expert", 2 * k) for k in range(1, chips)]

    early = jnp.concatenate(arrived[1:-1])
    chunks = [early] + [swap(early, "expert", 2 * k) for k in range(1, chips - 1)]
    *asked, early = lax.optimization_barrier((*asked, early))
    chunks.append(swap(early, "expert", 2 * (chips - 1)))

    pos = jnp.stack([place, shard])
    query, suffix_cache, early = lax.optimization_barrier((query, suffix_cache, early))
    partial = jax.ShapeDtypeStruct((2 * row_count * group_heads, LAT + LANES), bf16)
    partials = vmem_call(
        suffix_kernel,
        [partial] * chips,
        [
            pos,
            query.reshape(row_count, HEADS, KDIM),
            suffix_cache.reshape(row_count, SUFFIX, KDIM),
        ],
        4 * row_count * HEADS * SUFFIX * KDIM,
        scalars=1,
        scratch=[
            pltpu.VMEM((row_count, members, group_heads, partial.shape[1]), jnp.float32),
            pltpu.SMEM(suffix_count.shape, jnp.int32),
            pltpu.SemaphoreType.DMA,
        ],
        away=[suffix_count],
    )
    joined = jax.ShapeDtypeStruct((partial.shape[0], partial.shape[1] + PAIR), bf16)
    late = list(
        vmem_call(join_kernel, [joined] * chips, [arrived[-1]] + list(partials), piece.size)
    )
    late = [late[0]] + [swap(late[k], "expert", 2 * k) for k in range(1, chips)]

    rows = members * row_count * group_heads
    wide = jax.ShapeDtypeStruct((rows, WIDE), bf16)
    *queries, top, total, even, odd = vmem_call(
        functools.partial(first_kernel, variants, group_heads),
        [wide] * (2 * variants) + state_shapes(rows),
        [prefix_pool, swap(jnp.stack([part[1] for part in asked]), "expert", 1)]
        + asked,
        40 * rows * prefix_pool.size,
    )
    *chunks, late[1], late[2] = lax.optimization_barrier((*chunks, late[1], late[2]))
    held = vmem_call(
        pile_kernel,
        jax.ShapeDtypeStruct((chips * early.shape[0], early.shape[1]), bf16),
        chunks,
        chips * early.size,
    )
    chunks.append(swap(held, "expert", 1))
    state = vmem_call(
        functools.partial(middle_kernel, variants, list(range(1, holders - 1)), shard_blocks),
        state_shapes(rows),
        queries + [top, total, even, odd] + chunks,
        40 * rows * prefix_pool.size,
    )
    *held, top = lax.optimization_barrier((*late, state[0]))
    state = [top, *state[1:]]
    late = held + [swap(block, "expert", 1) for block in held]
    half = members * row_count // 2
    keep, away = vmem_call(
        functools.partial(last_kernel, variants, chips, holders - 1, shard_blocks),
        [
            jax.ShapeDtypeStruct((half, width), jnp.float32),
            jax.ShapeDtypeStruct((half, width), bf16),
        ],
        queries
        + list(state)
        + [arrival_order(chips, row_count, group_heads), value_up, out_proj]
        + late,
        4 * rows * prefix_pool.size + 4 * half * out_proj.size,
    )
    own, *sent = halve(keep, away, chips)
    sums = [swap(sent[k - 1], "expert", 2 * k) for k in reversed(range(1, chips))]
    residual_out, token_rows = vmem_call(
        norm_kernel,
        [
            jax.ShapeDtypeStruct((row_count, width), jnp.float32),
            jax.ShapeDtypeStruct((row_count, width + LANES), bf16),
        ],
        [hidden_in, norm_gain.reshape(1, width), expert_ids, gate_weights, own] + sums,
        10 * hidden_in.size,
    )

    blocks = spread(token_rows, members, holders)
    half = blocks[0].shape[0] * chips
    keep, away = vmem_call(
        expert_kernel,
        [
            jax.ShapeDtypeStruct((half, width), jnp.float32),
            jax.ShapeDtypeStruct((half, width), bf16),
        ],
        [pos] + blocks + [gate_proj, up_proj, down_proj],
        12 * half * gate_proj.size,
        scalars=1,
    )
    moe_sum = gather_sums(keep, away, members, holders)
    return (residual_out, moe_sum)


def solution(mesh):
    in_specs = (
        P(("dp", "expert"), None),
        P(("dp", "expert"), None),
        P("dp", None),
        P(("dp", "expert"), None),
        P(("dp", "expert"), None),
        P(("dp", "expert")),
        P(("dp", "expert")),
        P("expert", None, None),
        P("expert", None),
        P(),
        P(("dp", "expert"), None),
        P(("dp", "expert"), None),
        P("expert", None, "dp"),
        P("expert", None, "dp"),
        P("expert", "dp", None),
    )
    out_specs = (P(("dp", "expert"), None), P(("dp", "expert"), None))
    return jax.shard_map(
        per_device, mesh=mesh, in_specs=in_specs, out_specs=out_specs, check_vma=False
    )
```

```python
import functools

import jax
import jax.numpy as jnp
import numpy as np
from jax import lax
from jax.experimental import pallas as pl
from jax.experimental.pallas import tpu as pltpu
from jax.sharding import PartitionSpec as P

HEADS = 64
LAT = 512
TOPK = 6
BLOCK = 64
SUFFIX = 128
KDIM = 576


NEG_FILL = -1e30
SCORE_SCALE = 192.0 ** (-0.5)
NORM_EPS = 1e-06
LANES = 128
PAIR = 2 * KDIM
WIDE = KDIM + 64


def swap(value, axis, mask):
    size = lax.axis_size(axis)
    return lax.ppermute(value, axis, [(i, i ^ mask) for i in range(size)])


def dot(a, b, dims):
    return lax.dot_general(a, b, (dims, ((), ())), preferred_element_type=jnp.float32)


def vmem_call(kernel, out_shape, operands, flops, scalars=0, scratch=(), away=(), grant=16):
    specs = [pl.BlockSpec(memory_space=pltpu.SMEM)] * scalars
    specs += [pl.BlockSpec(memory_space=pltpu.VMEM)] * (len(operands) - scalars)
    specs += [pl.BlockSpec(memory_space=pl.ANY)] * len(away)
    size = sum(o.size * o.dtype.itemsize for o in operands)
    return pl.pallas_call(
        kernel,
        out_shape=out_shape,
        in_specs=specs,
        out_specs=jax.tree.map(lambda _: pl.BlockSpec(memory_space=pltpu.VMEM), out_shape),
        scratch_shapes=list(scratch),
        cost_estimate=pl.CostEstimate(flops=flops, bytes_accessed=size, transcendentals=0),
        compiler_params=pltpu.CompilerParams(vmem_limit_bytes=grant * 1024 * 1024),
    )(*operands, *away)


def suffix_kernel(pos, query_ref, keys_ref, count_hbm, *refs):
    outs, (rows, count, sem) = refs[:-3], refs[-3:]
    copy = pltpu.make_async_copy(count_hbm, count, sem)
    copy.start()
    place = pos[0]
    requests, heads, _ = query_ref.shape
    members = 2 * len(outs)
    group = heads // members
    all_scores = [
        dot(query_ref[r], keys_ref[r], ((1,), (1,))) * SCORE_SCALE for r in range(requests)
    ]
    copy.wait()
    for r in range(requests):
        scores = all_scores[r]
        live = lax.broadcasted_iota(jnp.int32, scores.shape, 1) < count[r]
        scores = jnp.where(live, scores, NEG_FILL)
        top = jnp.max(scores, axis=-1, keepdims=True).astype(jnp.bfloat16).astype(jnp.float32)
        weights = jnp.where(live, jnp.exp(scores - top), 0.0)
        total = jnp.sum(weights, axis=-1, keepdims=True)
        high = total.astype(jnp.bfloat16).astype(jnp.float32)
        numerator = dot(weights.astype(jnp.bfloat16), keys_ref[r, :, :LAT], ((1,), (0,)))
        lane = lax.broadcasted_iota(jnp.int32, (heads, LANES), 1)
        stats = jnp.where(lane == 0, top, jnp.where(lane == 1, high, total - high))
        full = jnp.concatenate([numerator, stats], axis=1)
        for g in range(members):
            rows[r, g] = full[g * group : (g + 1) * group]
    for k, out_ref in enumerate(outs):
        taken = [rows[r, place ^ (2 * k + s)] for s in range(2) for r in range(requests)]
        out_ref[...] = jnp.concatenate(taken, axis=0).astype(jnp.bfloat16)


def join_kernel(piece_ref, *refs):
    half = len(refs) // 2
    blocks = piece_ref.shape[0]
    for rows_ref, out_ref in zip(refs[:half], refs[half:]):
        width = rows_ref.shape[1]
        out_ref[:, :width] = rows_ref[...]
        for i in range(piece_ref.shape[1] // PAIR):
            out_ref[i * blocks : (i + 1) * blocks, width:] = piece_ref[:, i * PAIR : (i + 1) * PAIR]


def lane_pairs(refs, row):
    return [(ref, row, at) for ref in refs for at in range(0, ref.shape[1], PAIR)]


def stacked_pairs(refs, blocks):
    lane = refs[0].shape[1] - PAIR
    return [(ref, row, lane) for ref in refs for row in range(0, ref.shape[0], blocks)]


def pair_keys(pairs, blocks, spot):
    lane = lax.broadcasted_iota(jnp.int32, (blocks, LANES), 1)
    block = lax.broadcasted_iota(jnp.int32, (blocks, LANES), 0)
    first = (lane < 64).astype(jnp.float32).astype(jnp.bfloat16)
    last = (lane >= 64).astype(jnp.float32).astype(jnp.bfloat16)
    hot_even = (lane == 64 + spot + block).astype(jnp.float32).astype(jnp.bfloat16)
    hot_odd = (lane == spot + block).astype(jnp.float32).astype(jnp.bfloat16)
    even, odd = [], []
    for ref, row, at in pairs:
        keys = ref[row : row + blocks, at : at + PAIR]
        middle = keys[:, LAT : LAT + LANES]
        even.append(jnp.concatenate([keys[:, :LAT], middle * first + hot_even], axis=1))
        odd.append(jnp.concatenate([middle * last + hot_odd, keys[:, LAT + LANES :]], axis=1))
    return jnp.concatenate(even, axis=0), jnp.concatenate(odd, axis=0)


def advance(query_even, query_odd, even, odd, state):
    score_even = dot(query_even, even, ((1,), (1,))) * SCORE_SCALE
    score_odd = dot(query_odd, odd, ((1,), (1,))) * SCORE_SCALE
    top = jnp.maximum(
        jnp.max(score_even, axis=-1, keepdims=True), jnp.max(score_odd, axis=-1, keepdims=True)
    )
    if state is not None:
        top = jnp.maximum(top, state[0])
    weight_even = jnp.exp(score_even - top)
    weight_odd = jnp.exp(score_odd - top)
    total = jnp.sum(weight_even, axis=-1, keepdims=True)
    total = total + jnp.sum(weight_odd, axis=-1, keepdims=True)
    sum_even = dot(weight_even.astype(jnp.bfloat16), even[:, :LAT], ((1,), (0,)))
    sum_odd = dot(weight_odd.astype(jnp.bfloat16), odd, ((1,), (0,)))
    if state is not None:
        keep = jnp.exp(state[0] - top)
        total = total + state[1] * keep
        sum_even = sum_even + state[2] * keep
        sum_odd = sum_odd + state[3] * keep
    return top, total, sum_even, sum_odd


def put_state(state, refs):
    top_ref, total_ref, even_ref, odd_ref = refs
    top_ref[...] = jnp.broadcast_to(state[0], top_ref.shape)
    total_ref[...] = jnp.broadcast_to(state[1], total_ref.shape)
    even_ref[...] = state[2]
    odd_ref[...] = state[3]


def get_state(refs):
    return (refs[0][:, :1], refs[1][:, :1], refs[2][...], refs[3][...])


def state_shapes(rows):
    f32 = jnp.float32
    return [
        jax.ShapeDtypeStruct((rows, LANES), f32),
        jax.ShapeDtypeStruct((rows, LANES), f32),
        jax.ShapeDtypeStruct((rows, LAT), f32),
        jax.ShapeDtypeStruct((rows, WIDE), f32),
    ]


def first_kernel(variants, group, *refs):
    outs = refs[-4 - 2 * variants :]
    pool_ref, other_ref = refs[:2]
    mine = [ref[0] for ref in refs[2 : -4 - 2 * variants]]
    other = [other_ref[k] for k in range(other_ref.shape[0])]
    both = jnp.concatenate([p.astype(jnp.float32) for p in mine + other], axis=0)
    bias = both[:, group * KDIM :]
    rows = both.shape[0]
    lane = lax.broadcasted_iota(jnp.int32, (rows, LANES), 1)
    for v in range(variants):
        low = bias if v == 0 else pltpu.roll(bias, LANES - 64, 1)
        high = pltpu.roll(low, 64, 1)
        for h in range(group):
            at = h // 2 * PAIR
            if h % 2 == 0:
                wide = both[:, at : at + WIDE]
                last = jnp.where(lane < 64, wide[:, LAT:], high)
                even = jnp.concatenate([wide[:, :LAT], last], axis=1)
                odd = pltpu.roll(even, 64, 1)
            else:
                wide = both[:, at + LAT : at + PAIR]
                start = jnp.where(lane < 64, low, wide[:, :LANES])
                odd = jnp.concatenate([start, wide[:, LANES:]], axis=1)
                even = pltpu.roll(odd, WIDE - 64, 1)
            outs[2 * v][h * rows : (h + 1) * rows, :] = even.astype(jnp.bfloat16)
            outs[2 * v + 1][h * rows : (h + 1) * rows, :] = odd.astype(jnp.bfloat16)
    even, odd = pair_keys(lane_pairs([pool_ref], 0), pool_ref.shape[0], 0)
    put_state(advance(outs[0][...], outs[1][...], even, odd, None), outs[2 * variants :])


def walk(queries, sources, blocks, state):
    for q, pairs in sources:
        variant, spot = divmod(q * blocks, 64)
        even, odd = pair_keys(pairs, blocks, spot)
        query_even, query_odd = queries[2 * variant : 2 * variant + 2]
        state = advance(query_even[...], query_odd[...], even, odd, state)
    return state


def middle_kernel(variants, sources, blocks, *refs):
    queries, refs = refs[: 2 * variants], refs[2 * variants :]
    state, chunks, outs = refs[:4], refs[4:-4], refs[-4:]
    each = chunks[0].shape[0]
    places = [(ref, row) for ref in chunks for row in range(0, ref.shape[0], each)]
    sources = [
        (q, [pair for ref, row in places for pair in lane_pairs([ref], row + i * blocks)])
        for i, q in enumerate(sources)
    ]
    put_state(walk(queries, sources, blocks, get_state(state)), outs)


def last_kernel(variants, chips, source, blocks, *refs):
    queries, refs = refs[: 2 * variants], refs[2 * variants :]
    state, refs = refs[:4], refs[4:]
    order_ref, value_ref, proj_ref = refs[:3]
    chunks, (keep_ref, away_ref) = refs[3:-2], refs[-2:]
    half = chunks[0].shape[0] // 2
    own = []
    for k in range(chips):
        own.append(chunks[k][:half, : LAT + LANES].astype(jnp.float32))
        own.append(chunks[chips + k][half:, : LAT + LANES].astype(jnp.float32))
    own = dot(order_ref[...], jnp.concatenate(own, axis=0).astype(jnp.bfloat16), ((1,), (0,)))
    sources = [(source, stacked_pairs(chunks, blocks))]
    top, total, even, odd = walk(queries, sources, blocks, get_state(state))
    stats = own[:, LAT:]
    own_top = stats[:, 0:1]
    new_top = jnp.maximum(top, own_top)
    keep = jnp.exp(top - new_top)
    own_keep = jnp.exp(own_top - new_top)
    total = total * keep + (stats[:, 1:2] + stats[:, 2:3]) * own_keep
    numerator = (even + odd[:, 64 : 64 + LAT]) * keep
    numerator = numerator + own[:, :LAT] * own_keep
    context = (numerator / total).astype(jnp.bfloat16)
    heads = value_ref.shape[0]
    rows = context.shape[0] // heads
    values = [
        dot(context[h * rows : (h + 1) * rows], value_ref[h], ((1,), (0,))).astype(jnp.bfloat16)
        for h in range(heads)
    ]
    values = jnp.concatenate(values, axis=1)
    step = 1024
    half = rows // 2
    for at in range(0, proj_ref.shape[1], step):
        part = dot(values, proj_ref[:, at : at + step], ((1,), (0,)))
        keep_ref[:, at : at + step] = part[:half]
        away_ref[:, at : at + step] = part[half:].astype(jnp.bfloat16)


def expert_kernel(pos, *refs):
    blocks, (gate_ref, up_ref, down_ref, keep_ref, away_ref) = refs[:-5], refs[-5:]
    width = down_ref.shape[2]
    rows = jnp.concatenate([b[:, :width] for b in blocks], axis=0)
    gates = jnp.concatenate([b[:, width:] for b in blocks], axis=0).astype(jnp.float32)
    lane = lax.broadcasted_iota(jnp.int32, gates.shape, 1)
    gate = jnp.sum(jnp.where(lane == pos[0], gates, 0.0), axis=1, keepdims=True)
    gate_part = dot(rows, gate_ref[0], ((1,), (0,)))
    up_part = dot(rows, up_ref[0], ((1,), (0,)))
    hidden = (gate_part / (1.0 + jnp.exp(-gate_part)) * up_part).astype(jnp.bfloat16)
    half = rows.shape[0] // 2
    step = 1024
    for at in range(0, width, step):
        part = dot(hidden, down_ref[0, :, at : at + step], ((1,), (0,))) * gate
        keep_ref[:, at : at + step] = part[:half].astype(keep_ref.dtype)
        away_ref[:, at : at + step] = part[half:].astype(jnp.bfloat16)


def halve_kernel(keep_ref, away_ref, *outs):
    rows = outs[0].shape[0]
    for k, out_ref in enumerate(outs):
        at = pl.ds(k * rows, rows)
        total = keep_ref[at, :].astype(jnp.float32) + away_ref[at, :].astype(jnp.float32)
        out_ref[...] = total.astype(out_ref.dtype)


def norm_kernel(hidden_ref, gain_ref, ids_ref, weight_ref, own_ref, *refs):
    arrived, (residual_ref, row_ref) = refs[:-2], refs[-2:]
    width = hidden_ref.shape[1]
    total = own_ref[...]
    for ref in arrived:
        total = total + ref[...].astype(jnp.float32)
    total = hidden_ref[...].astype(jnp.float32) + total
    residual_ref[...] = total
    scale = lax.rsqrt(jnp.mean(total * total, axis=-1, keepdims=True) + NORM_EPS)
    row_ref[:, :width] = (total * scale * gain_ref[...].astype(jnp.float32)).astype(jnp.bfloat16)
    lane = lax.broadcasted_iota(jnp.int32, (total.shape[0], LANES), 1)
    ids, weights = ids_ref[...], weight_ref[...].astype(jnp.float32)
    gates = jnp.zeros(lane.shape, jnp.float32)
    for j in range(TOPK):
        gates = gates + jnp.where(lane == ids[:, j : j + 1], weights[:, j : j + 1], 0.0)
    row_ref[:, width:] = gates.astype(jnp.bfloat16)


def pile_kernel(*refs):
    rows = refs[0].shape[0]
    for i, ref in enumerate(refs[:-1]):
        refs[-1][i * rows : (i + 1) * rows, :] = ref[...]


def stack_kernel(*refs):
    rows = jnp.concatenate([ref[...].astype(jnp.float32) for ref in refs[:-1]], axis=0)
    refs[-1][...] = rows.astype(jnp.bfloat16)


def halve(keep, away, blocks):
    rows, width = keep.shape[0] // blocks, keep.shape[1]
    shapes = [jax.ShapeDtypeStruct((rows, width), jnp.float32)]
    shapes += [jax.ShapeDtypeStruct((rows, width), jnp.bfloat16)] * (blocks - 1)
    return vmem_call(halve_kernel, shapes, [keep, swap(away, "expert", 1)], keep.size)


def spread(rows, members, holders):
    by_z = [swap(rows, "dp", q) for q in reversed(range(1, holders))]
    by_z = [rows] + by_z[::-1]
    shape = jax.ShapeDtypeStruct((holders * rows.shape[0], rows.shape[1]), rows.dtype)
    by_z = vmem_call(stack_kernel, shape, by_z, rows.size)
    blocks = [swap(by_z, "expert", 2 * k) for k in reversed(range(1, members // 2))]
    blocks = [by_z] + blocks[::-1]
    return blocks + [swap(block, "expert", 1) for block in blocks]


def gather_sums(keep, away, members, holders):
    chips = members // 2
    rows, width = keep.shape[0] // chips, keep.shape[1]
    total, *sent = halve(keep, away, chips)
    for k in reversed(range(1, chips)):
        total = total + swap(sent[k - 1], "expert", 2 * k).astype(jnp.float32)
    total = total.reshape(holders, rows // holders, width)
    sent = total.astype(jnp.bfloat16)
    result = total[0]
    for q in reversed(range(1, holders)):
        result = result + swap(sent[q], "dp", q).astype(jnp.float32)
    return result


def arrival_order(chips, requests, heads):
    source = np.arange(chips * 2 * requests * heads).reshape(chips, 2, requests, heads)
    source = source.transpose(3, 1, 0, 2).reshape(-1)
    order = np.zeros((source.size, source.size), np.float32)
    order[np.arange(source.size), source] = 1.0
    return jnp.asarray(order, jnp.bfloat16)


def per_device(
    hidden_in,
    query,
    prefix_pool,
    suffix_cache,
    block_list,
    prefix_count,
    suffix_count,
    value_up,
    out_proj,
    norm_gain,
    expert_ids,
    gate_weights,
    gate_proj,
    up_proj,
    down_proj,
):
    bf16 = jnp.bfloat16
    row_count, width = hidden_in.shape
    members = lax.axis_size("expert")
    holders = lax.axis_size("dp")
    chips = members // 2
    place = lax.axis_index("expert")
    shard = lax.axis_index("dp")
    shard_blocks = prefix_pool.shape[0]
    total_blocks = shard_blocks * holders

    piece_width = prefix_pool.shape[1] // members
    piece = lax.dynamic_slice_in_dim(prefix_pool, place * piece_width, piece_width, 1)
    arrived = [None] * holders
    for q in sorted(range(1, holders), key=lambda q: (bin(q).count("1"), q)):
        low = q & -q
        arrived[q] = swap(piece if q == low else arrived[q ^ low], "dp", low)

    group_heads = HEADS // members
    variants = -(-total_blocks // 64)
    in_prefix = jnp.arange(block_list.shape[1], dtype=jnp.int32)[None, :] < prefix_count[:, None]
    slots = jnp.arange(LANES, dtype=jnp.int32)
    ids = (shard ^ (slots // shard_blocks)) * shard_blocks + slots % shard_blocks
    member = jnp.any((block_list[:, :, None] == ids) & in_prefix[:, :, None], axis=1)
    bias = jnp.where(member, 0.0, NEG_FILL).astype(bf16)
    group_width = group_heads * KDIM
    asked = []
    for k in range(chips):
        pair = [
            lax.dynamic_slice_in_dim(query, (place ^ j) * group_width, group_width, 1)
            for j in (2 * k, 2 * k + 1)
        ]
        asked.append(jnp.stack([jnp.concatenate([part, bias], axis=1) for part in pair]))
    asked = [asked[0]] + [swap(asked[k], "expert", 2 * k) for k in range(1, chips)]

    early = jnp.concatenate(arrived[1:-1])
    chunks = [early] + [swap(early, "expert", 2 * k) for k in range(1, chips - 1)]
    *asked, early = lax.optimization_barrier((*asked, early))
    chunks.append(swap(early, "expert", 2 * (chips - 1)))

    pos = jnp.stack([place, shard])
    query, suffix_cache, early = lax.optimization_barrier((query, suffix_cache, early))
    partial = jax.ShapeDtypeStruct((2 * row_count * group_heads, LAT + LANES), bf16)
    partials = vmem_call(
        suffix_kernel,
        [partial] * chips,
        [
            pos,
            query.reshape(row_count, HEADS, KDIM),
            suffix_cache.reshape(row_count, SUFFIX, KDIM),
        ],
        4 * row_count * HEADS * SUFFIX * KDIM,
        scalars=1,
        scratch=[
            pltpu.VMEM((row_count, members, group_heads, partial.shape[1]), jnp.float32),
            pltpu.SMEM(suffix_count.shape, jnp.int32),
            pltpu.SemaphoreType.DMA,
        ],
        away=[suffix_count],
    )
    joined = jax.ShapeDtypeStruct((partial.shape[0], partial.shape[1] + PAIR), bf16)
    late = list(
        vmem_call(join_kernel, [joined] * chips, [arrived[-1]] + list(partials), piece.size)
    )
    late = [late[0]] + [swap(late[k], "expert", 2 * k) for k in range(1, chips)]

    rows = members * row_count * group_heads
    wide = jax.ShapeDtypeStruct((rows, WIDE), bf16)
    *queries, top, total, even, odd = vmem_call(
        functools.partial(first_kernel, variants, group_heads),
        [wide] * (2 * variants) + state_shapes(rows),
        [prefix_pool, swap(jnp.stack([part[1] for part in asked]), "expert", 1)]
        + asked,
        40 * rows * prefix_pool.size,
    )
    *chunks, late[1], late[2] = lax.optimization_barrier((*chunks, late[1], late[2]))
    held = vmem_call(
        pile_kernel,
        jax.ShapeDtypeStruct((chips * early.shape[0], early.shape[1]), bf16),
        chunks,
        chips * early.size,
    )
    chunks.append(swap(held, "expert", 1))
    state = vmem_call(
        functools.partial(middle_kernel, variants, list(range(1, holders - 1)), shard_blocks),
        state_shapes(rows),
        queries + [top, total, even, odd] + chunks,
        40 * rows * prefix_pool.size,
    )
    late[-1], top = lax.optimization_barrier((late[-1], state[0]))
    state = [top, *state[1:]]
    late += [swap(block, "expert", 1) for block in late]
    half = members * row_count // 2
    keep, away = vmem_call(
        functools.partial(last_kernel, variants, chips, holders - 1, shard_blocks),
        [
            jax.ShapeDtypeStruct((half, width), jnp.float32),
            jax.ShapeDtypeStruct((half, width), bf16),
        ],
        queries
        + list(state)
        + [arrival_order(chips, row_count, group_heads), value_up, out_proj]
        + late,
        4 * rows * prefix_pool.size + 4 * half * out_proj.size,
    )
    own, *sent = halve(keep, away, chips)
    sums = [swap(sent[k - 1], "expert", 2 * k) for k in reversed(range(1, chips))]
    residual_out, token_rows = vmem_call(
        norm_kernel,
        [
            jax.ShapeDtypeStruct((row_count, width), jnp.float32),
            jax.ShapeDtypeStruct((row_count, width + LANES), bf16),
        ],
        [hidden_in, norm_gain.reshape(1, width), expert_ids, gate_weights, own] + sums,
        10 * hidden_in.size,
    )

    blocks = spread(token_rows, members, holders)
    half = blocks[0].shape[0] * chips
    keep, away = vmem_call(
        expert_kernel,
        [
            jax.ShapeDtypeStruct((half, width), jnp.float32),
            jax.ShapeDtypeStruct((half, width), bf16),
        ],
        [pos] + blocks + [gate_proj, up_proj, down_proj],
        12 * half * gate_proj.size,
        scalars=1,
    )
    moe_sum = gather_sums(keep, away, members, holders)
    return (residual_out, moe_sum)


def solution(mesh):
    in_specs = (
        P(("dp", "expert"), None),
        P(("dp", "expert"), None),
        P("dp", None),
        P(("dp", "expert"), None),
        P(("dp", "expert"), None),
        P(("dp", "expert")),
        P(("dp", "expert")),
        P("expert", None, None),
        P("expert", None),
        P(),
        P(("dp", "expert"), None),
        P(("dp", "expert"), None),
        P("expert", None, "dp"),
        P("expert", None, "dp"),
        P("expert", "dp", None),
    )
    out_specs = (P(("dp", "expert"), None), P(("dp", "expert"), None))
    return jax.shard_map(
        per_device, mesh=mesh, in_specs=in_specs, out_specs=out_specs, check_vma=False
    )
```
